128 devices in a mesh: frame: 2 (over core), video: 32 (over z, y, x_hi), score: 2 (over x_lo).
Axes of the slice: x: 4 (x_hi: 2, x_lo: 2; x = x_hi * 2 + x_lo), y: 4, z: 4, core: 2. Of those that a mesh axis runs over, the one named last changes fastest.
Arguments:
- queries: bfloat16 [2, 32, 512, 5120], P('frame', 'video', None, 'score'), may hold values from -120 to 120
- key_states: bfloat16 [2, 32, 512, 5120], P('frame', 'video', None, 'score'), may hold values from -4 to 4, as said below
- value_states: bfloat16 [2, 32, 512, 5120], P('frame', 'video', None, 'score'), may hold values from -32 to 32
- out_proj: bfloat16 [5120, 5120], P('score'), may hold values from -0.078125 to 0.078125
- noise_field: bfloat16 [2, 32, 512, 5120], P('frame', 'video', 'score'), may hold values from -6 to 6
- timesteps: int32 [2, 32], P('frame', 'video'), may hold values from 20 to 699
- routes: int32 [2, 32, 512, 1], P('frame', 'video', 'score'), may hold values from 0 to 63; in each aligned block of 256 rows (0 to 255, 256 to 511, ..., all dimensions but the last counted through in order) at most 8 rows name the same one
- modulation: float32 [64, 2, 5120], P(('video', 'score')), may hold values from -3 to 3
- context: float32 [32, 2, 5120], replicated, may hold values from -6 to 6
- guidance: float32 [32], replicated, may hold values from 1.5 to 6
- head_proj: bfloat16 [64, 5120, 64], P(('video', 'score')), may hold values from -0.078125 to 0.078125
Outputs:
- student_rows: bfloat16 [2, 32, 512, 5120], P('frame', 'video', 'score')
- guided_score: bfloat16 [2, 32, 512, 64], P('frame', 'video', 'score')
The draws below stay inside these ranges and needn't reach their ends.
Inputs may be any that keep to these rules, and one draw needn't show every extreme that they name: `key_states`: row 1 of some blocks may nearly repeat row 0 of the same block. `routes`: among the 256 rows of one device no scorer appears more than 8 times.
All inputs are finite; a program needn't handle non-finite values.
Results may differ from the reference program's by a relative error of at most 0.014.
Values may be sent and summed in bfloat16 or wider, within the bound.
No kernel may reach another device: no remote copies, remote signals or barrier semaphores. Data moves between devices by JAX's collectives and lax.ppermute only.
A program may use at most 192 MiB of HBM per device.

```python
import math
import jax
import jax.numpy as jnp
import numpy as np
from jax import lax

D = 5120
HEADS = 40
HEAD_DIM = 128
OUT = 64
TOK = 512
BLOCKS = 2
VIDEOS = 32
SCORERS = 64
ROWS = 256
CAP = 8
N_SCORE = 2


def base_keys(key):
    return jax.random.truncated_normal(key, -4.0, 4.0, (BLOCKS, VIDEOS, TOK, D), jnp.float32)


def draw_key_states(key, part):
    base = base_keys(key)
    return base.astype(jnp.bfloat16)


def draw_queries(key, part):
    own_key = jax.random.fold_in(key, 5)
    drawn = jax.random.truncated_normal(own_key, -4.0, 4.0, (BLOCKS, VIDEOS, TOK, D), jnp.float32)
    return drawn.astype(jnp.bfloat16)


def with_ends(array, rng, low, high):
    longest = array.shape.index(max(array.shape))
    spots = []
    for shift in (0, 1):
        where = [jax.random.randint(jax.random.fold_in(rng, axis), (), 0, length) for axis, length in enumerate(array.shape)]
        where[longest] = (where[longest] + shift) % array.shape[longest]
        spots.append(tuple(where))
    return array.at[spots[0]].set(low).at[spots[1]].set(high)


def levels(rng, dims, shards, smallest, top_value):
    level, own = 1.0, jax.random.fold_in(rng, 6)
    for axis_at, shards_of in shards:
        heights = jnp.exp(jax.random.uniform(jax.random.fold_in(own, axis_at), (shards_of,), jnp.float32, smallest / len(shards), top_value / len(shards)))
        level = level * jnp.repeat(heights, dims[axis_at] // shards_of).reshape([-1 if axis == axis_at else 1 for axis in range(len(dims))])
    return level


def deal_out(key, own, number, rows, number_of, top, reach, lean):
    order = jax.random.permutation(key, number_of)
    packed, ordinary = shares(number_of, rows * top, reach, lean, True), shares(number_of, rows * top, reach, lean, False)
    places = jnp.arange(number_of)

    def named(tallies, rotation):
        used = int((tallies > 0).sum())
        fixed = max(1, used // 4)
        shifted = fixed + (places - fixed + rotation * (used - fixed)) % max(1, number_of - fixed)
        return jnp.zeros((number_of,), jnp.int32).at[order[jnp.where(places < fixed, places, shifted)]].set(jnp.asarray(tallies, jnp.int32))

    tallies = jnp.where(number % 4 == 0, named(packed, number // 4), named(ordinary, number - number // 4 - 1))
    mixed = jax.random.permutation(jax.random.fold_in(own, 3), number_of)
    source_of, taker = mixed[0:number_of // 2 * 2:2], mixed[1:number_of // 2 * 2:2]
    slack = jnp.minimum(tallies[source_of] - 1, reach - tallies[taker]) // 2
    slack = jnp.where((source_of == order[0]) | (taker == order[0]) | (tallies[taker] == 0), 0, jnp.maximum(slack, 0))
    shifted = jax.random.randint(jax.random.fold_in(own, 4), (number_of // 2,), 0, 1 << 20) % (slack + 1)
    tallies = tallies.at[source_of].add(-shifted).at[taker].add(shifted)
    members = jnp.searchsorted(jnp.cumsum(tallies), jnp.arange(rows * top), side="right").astype(jnp.int32)
    grid = members.reshape(top, rows).T
    grid = grid[jax.random.permutation(jax.random.fold_in(own, 1), rows)]
    rotation = jax.random.randint(jax.random.fold_in(own, 2), (rows, 1), 0, top)
    return jnp.take_along_axis(grid, (jnp.arange(top)[None, :] + rotation) % top, axis=1)


def shares(number_of, total, bound, slope, full):
    loads = [(1 << 20) // math.isqrt(grade ** slope) + 1 for grade in range(1, number_of + 1)]
    largest = bound if full else min(bound, max(-(-total // number_of), total * loads[0] // sum(loads)))
    least = 1 if total - largest >= number_of - 1 else 0
    given, rest = [largest] + [least] * (number_of - 1), total - largest - least * (number_of - 1)
    while rest > 0:
        candidates = [i for i in range(1, number_of) if given[i] < largest] or [i for i in range(1, number_of) if given[i] < bound]
        pool, left = sum([loads[i] for i in candidates]), rest
        for i in candidates:
            more = min(bound - given[i], max(1, left * loads[i] // pool), rest)
            given[i] = given[i] + more
            rest = rest - more
    return np.array(given)


def scatter_about(rng, shape, deviation, most, split=(), held_as=jnp.bfloat16):
    drawn = jax.random.normal(rng, shape, jnp.float32) * deviation
    if len(split) > 0:
        drawn = levels(rng, shape, split, -0.22, 0.18) * drawn
    return jnp.clip(drawn, min=-most, max=most).astype(held_as)


def setup_inputs(seed: int = 0) -> dict:
    seeds = jax.random.split(jax.random.key(seed), 12)
    queries = draw_queries(jax.random.fold_in(seeds[11], 71), 0)
    key_states = draw_key_states(jax.random.fold_in(seeds[11], 71), 0)
    value_states = scatter_about(seeds[2], (BLOCKS, VIDEOS, TOK, D), ((TOK * BLOCKS) ** 0.5 / 4), 32.0, ((0, 2), (1, 32), (3, 2)))
    out_proj = scatter_about(seeds[3], (D, D), D ** -0.5, 0.078125, ((0, 2),))
    noise_field = scatter_about(seeds[4], (BLOCKS, VIDEOS, TOK, D), 1.0, 6.0, ((0, 2), (1, 32), (2, 2)))
    timesteps = with_ends(jax.random.randint(seeds[5], (BLOCKS, VIDEOS), 20, 700), jax.random.fold_in(seeds[5], 1), 20, 699).astype(jnp.int32)
    routes_keys = jax.random.split(jax.random.fold_in(seeds[6], 1), BLOCKS * VIDEOS * TOK // ROWS)
    routes_turns = jax.random.permutation(jax.random.fold_in(seeds[6], 3), BLOCKS * VIDEOS * TOK // ROWS)
    routes = jax.vmap(lambda own, number: deal_out(jax.random.fold_in(seeds[6], 2), own, number, ROWS, SCORERS, 1, CAP, 1))(routes_keys, routes_turns).reshape((BLOCKS, VIDEOS, TOK, 1))
    modulation = scatter_about(seeds[7], (SCORERS, 2, D), 0.5, 3.0, ((0, 64),), jnp.float32)
    context = scatter_about(seeds[8], (VIDEOS, 2, D), 1.0, 6.0, (), jnp.float32)
    guidance = jnp.clip(jnp.exp(jax.random.uniform(seeds[9], (VIDEOS,), jnp.float32, math.log(1.5), math.log(6.0))), 1.5, 6.0)
    head_proj = scatter_about(seeds[10], (SCORERS, D, OUT), D ** -0.5, 0.078125, ((0, 64),))
    return {"queries": queries, "key_states": key_states, "value_states": value_states, "out_proj": out_proj, "noise_field": noise_field, "timesteps": timesteps, "routes": routes, "modulation": modulation, "context": context, "guidance": guidance, "head_proj": head_proj}


def attend_block(block_index, queries, key_states, value_states):
    count = block_index + 1
    query_heads = jnp.moveaxis(queries[block_index].reshape(VIDEOS, TOK, HEADS, HEAD_DIM), 2, 0)
    key_heads = jnp.moveaxis(key_states[:count].reshape(count, VIDEOS, TOK, HEADS, HEAD_DIM), 3, 0)
    value_heads = jnp.moveaxis(value_states[:count].reshape(count, VIDEOS, TOK, HEADS, HEAD_DIM), 3, 0)

    def one_head(operands):
        query_one, key_one, value_one = operands
        key_flat = jnp.moveaxis(key_one, 0, 1).reshape(VIDEOS, count * TOK, HEAD_DIM)
        value_flat = jnp.moveaxis(value_one, 0, 1).reshape(VIDEOS, count * TOK, HEAD_DIM)
        scores = jnp.einsum('vqd,vkd->vqk', query_one.astype(jnp.float32), key_flat.astype(jnp.float32)) * HEAD_DIM ** (-0.5)
        row_peak = lax.optimization_barrier(jnp.max(scores, axis=-1, keepdims=True))
        soft_exp = jnp.exp(scores - row_peak)
        row_total = lax.optimization_barrier(jnp.sum(soft_exp, axis=-1, keepdims=True))
        rounded = lax.optimization_barrier(soft_exp.astype(jnp.bfloat16)).astype(jnp.float32)
        return jnp.einsum('vqk,vkd->vqd', rounded, value_flat.astype(jnp.float32)) / row_total
    result = lax.map(one_head, (query_heads, key_heads, value_heads))
    return jnp.moveaxis(result, 0, 2).reshape(VIDEOS, TOK, D)

def reference(queries, key_states, value_states, out_proj, noise_field, timesteps, routes, modulation, context, guidance, head_proj):
    attended = jnp.stack([attend_block(index, queries, key_states, value_states) for index in range(BLOCKS)]).astype(jnp.bfloat16)
    group_width = D // N_SCORE
    flat_rows = attended.reshape(BLOCKS * VIDEOS * TOK, N_SCORE, group_width)
    summed = jnp.zeros((BLOCKS * VIDEOS * TOK, D), jnp.float32)
    for group in range(N_SCORE):
        partial_value = jnp.dot(flat_rows[:, group], out_proj[group * group_width:(group + 1) * group_width], preferred_element_type=jnp.float32)
        summed = summed + lax.optimization_barrier(partial_value.astype(jnp.bfloat16)).astype(jnp.float32)
    student_rows = summed.astype(jnp.bfloat16).reshape(BLOCKS, VIDEOS, TOK, D)
    noise_level = (timesteps.astype(jnp.float32) / 1000.0)[:, :, None, None]
    noisy = ((1.0 - noise_level) * student_rows.astype(jnp.float32) + noise_level * noise_field.astype(jnp.float32)).astype(jnp.bfloat16)
    head_wide = head_proj.astype(jnp.float32)

    def score_block(operands):
        block_rows, targets = operands
        hidden = block_rows.astype(jnp.float32)[:, :, None, :] + context[:, None, :, :]
        normed = hidden * lax.rsqrt(lax.optimization_barrier(jnp.mean(hidden * hidden, axis=-1, keepdims=True)) + 1e-06)
        bucket_mod = modulation[targets]
        shaped = (normed * (1.0 + bucket_mod[:, :, 0:1, :]) + bucket_mod[:, :, 1:2, :]).astype(jnp.bfloat16)
        every_head = jnp.einsum('vtcd,sdo->vtcso', shaped.astype(jnp.float32), head_wide)
        chosen = (targets[:, :, None] == jnp.arange(SCORERS, dtype=jnp.int32)[None, None, :]).astype(jnp.float32)
        projected = jnp.einsum('vtcso,vts->vtco', every_head, chosen)
        conditional = projected[:, :, 0]
        unconditional = projected[:, :, 1]
        return (unconditional + guidance[:, None, None] * (conditional - unconditional)).astype(jnp.bfloat16)
    guided_score = lax.map(score_block, (noisy, routes[..., 0]))
    return (student_rows, guided_score)
```

```python
import functools
import math

import jax
import jax.numpy as jnp
from jax import lax
from jax.experimental import pallas as pl
from jax.experimental.pallas import tpu as pltpu
from jax.sharding import Mesh
from jax.sharding import PartitionSpec as P

HEAD_DIM = 128
CHUNKS = 4
HEAD_GROUP = 5
SCALE2 = HEAD_DIM ** (-0.5) * math.log2(math.e)
NT = (((1,), (1,)), ((), ()))
NN = (((1,), (0,)), ((), ()))


def dot_nt(a, b):
    return lax.dot_general(a, b, NT, preferred_element_type=jnp.float32)


def dot_nn(a, b):
    return lax.dot_general(a, b, NN, preferred_element_type=jnp.float32)


def attend_kernel(info, q_ref, k_ref, v_ref, ke_ref, ve_ref, o_ref):
    later = info[1] == 1
    for h in range(HEAD_GROUP):
        cols = slice(h * HEAD_DIM, (h + 1) * HEAD_DIM)

        @pl.when(later)
        def both():
            q = q_ref[:, cols]
            s_own = dot_nt(q, k_ref[:, cols])
            s_early = dot_nt(q, ke_ref[:, cols])
            peak = jnp.maximum(
                jnp.max(s_own, axis=1, keepdims=True), jnp.max(s_early, axis=1, keepdims=True)
            )
            p_own = jnp.exp2((s_own - peak) * SCALE2)
            p_early = jnp.exp2((s_early - peak) * SCALE2)
            total = jnp.sum(p_own, axis=1, keepdims=True) + jnp.sum(p_early, axis=1, keepdims=True)
            acc = dot_nn(p_own.astype(jnp.bfloat16), v_ref[:, cols]) + dot_nn(
                p_early.astype(jnp.bfloat16), ve_ref[:, cols]
            )
            o_ref[:, cols] = (acc / total).astype(jnp.bfloat16)

        @pl.when(jnp.logical_not(later))
        def own():
            s_own = dot_nt(q_ref[:, cols], k_ref[:, cols])
            peak = jnp.max(s_own, axis=1, keepdims=True)
            p_own = jnp.exp2((s_own - peak) * SCALE2)
            total = jnp.sum(p_own, axis=1, keepdims=True)
            acc = dot_nn(p_own.astype(jnp.bfloat16), v_ref[:, cols])
            o_ref[:, cols] = (acc / total).astype(jnp.bfloat16)


def attend(half, frame, queries, keys, values, keys_early, values_early):
    tok, width = queries.shape
    rows = tok // 2
    wide = HEAD_GROUP * HEAD_DIM
    whole = pl.BlockSpec((tok, wide), lambda i, info: (0, i))
    return pl.pallas_call(
        attend_kernel,
        grid_spec=pltpu.PrefetchScalarGridSpec(
            num_scalar_prefetch=1,
            grid=(width // wide,),
            in_specs=[pl.BlockSpec((rows, wide), lambda i, info: (info[0], i))] + [whole] * 4,
            out_specs=pl.BlockSpec((rows, wide), lambda i, info: (0, i)),
        ),
        out_shape=jax.ShapeDtypeStruct((rows, width), jnp.bfloat16),
        compiler_params=pltpu.CompilerParams(vmem_limit_bytes=40 * 1024 * 1024),
        cost_estimate=pl.CostEstimate(
            flops=6 * rows * tok * width, bytes_accessed=5 * tok * width * 2, transcendentals=0
        ),
        name="attend",
    )(jnp.stack([half, frame]).astype(jnp.int32), queries, keys, values, keys_early, values_early)


def split3(x):
    high = lax.reduce_precision(x, 8, 7)
    rest = x - high
    mid = lax.reduce_precision(rest, 8, 7)
    low = rest - mid
    return high.astype(jnp.bfloat16), mid.astype(jnp.bfloat16), low.astype(jnp.bfloat16)


def shards(
    queries,
    key_states,
    value_states,
    out_proj,
    noise_field,
    timesteps,
    routes,
    modulation,
    context,
    guidance,
    head_proj,
):
    frame = lax.axis_index("frame")
    xl = lax.axis_index("xl")
    xh = lax.axis_index("xh")
    y_at = lax.axis_index("y")
    z_at = lax.axis_index("z")
    z_count = lax.axis_size("z")
    q, k, v = queries[0, 0], key_states[0, 0], value_states[0, 0]
    width = out_proj.shape[1]
    half_rows = q.shape[0] // 2
    chunk = width // CHUNKS
    swap = [(0, 1), (1, 0)]

    k_early = lax.ppermute(k, "frame", [(0, 1)])
    v_early = lax.ppermute(v, "frame", [(0, 1)])

    head = head_proj[0].astype(jnp.float32)
    out_count = head.shape[1]
    feats = out_count // 2
    scaled = jnp.transpose(head * (1.0 + modulation[0, 0])[:, None]).astype(jnp.bfloat16)
    shift_out = jnp.sum(head * modulation[0, 1][:, None], axis=0)
    extra = jnp.stack(split3(shift_out), axis=1)
    extra = jnp.pad(extra, ((0, 0), (0, 125)))
    packed = jnp.concatenate([scaled, extra], axis=1)
    mine = lax.dynamic_slice_in_dim(packed, frame * feats, feats, 0)
    heads_own = lax.all_gather(mine, ("y", "xh", "xl"), axis=0, tiled=True)
    heads_other = lax.ppermute(heads_own, "frame", swap)
    group = heads_own.shape[0] // feats

    targets = routes[0, 0, :, 0]
    towards = lax.rem(targets // group - z_at + z_count, z_count)
    local = lax.rem(targets, group)
    slots = group * 8
    same = towards[:, None] == towards[None, :]
    at = jnp.arange(half_rows, dtype=jnp.int32)
    rank = jnp.sum((same & (at[:, None] > at[None, :])).astype(jnp.int32), axis=1)
    place = towards * slots + rank
    picker = (place[None, :] == jnp.arange(z_count * slots, dtype=jnp.int32)[:, None]).astype(
        jnp.bfloat16
    )

    part_far = attend(1 - xl, frame, q, k, v, k_early, v_early)
    arrived = []
    for c in range(CHUNKS):
        w = out_proj[:, c * chunk : (c + 1) * chunk]
        arrived.append(lax.ppermute(dot_nn(part_far, w).astype(jnp.bfloat16), "xl", swap))
    part_own = attend(xl, frame, q, k, v, k_early, v_early)
    kept = [
        dot_nn(part_own, out_proj[:, c * chunk : (c + 1) * chunk]).astype(jnp.bfloat16)
        for c in range(CHUNKS)
    ]

    noise_level = timesteps[0, 0].astype(jnp.float32) / 1000.0
    z_from = [lax.rem(z_at - d + z_count, z_count) for d in range(z_count)]
    videos = jnp.stack([(z * 4 + y_at) * 2 + xh for z in z_from])
    ctx = context[videos]
    weight = guidance[videos]
    ctx_pieces = jnp.stack(split3(ctx)).reshape(3 * z_count * 2, width)

    student = []
    y_own = y_other = 0.0
    b_own = b_other = 0.0
    squares = 0.0
    ids = None
    for c in range(CHUNKS):
        cols = slice(c * chunk, (c + 1) * chunk)
        rows = (kept[c].astype(jnp.float32) + arrived[c].astype(jnp.float32)).astype(jnp.bfloat16)
        student.append(rows)
        noisy = (
            (1.0 - noise_level) * rows.astype(jnp.float32)
            + noise_level * noise_field[0, 0][:, cols].astype(jnp.float32)
        ).astype(jnp.bfloat16)
        if c == 0:
            tag = jnp.pad(local.astype(jnp.bfloat16)[:, None], ((0, 0), (0, 127)))
            noisy = jnp.concatenate([noisy, tag], axis=1)
        picked = dot_nn(picker, noisy).astype(jnp.bfloat16).reshape(z_count, slots, noisy.shape[1])
        blocks = [picked[0]]
        for d in range(1, z_count):
            blocks.append(
                lax.ppermute(picked[d], "z", [(j, (j + d) % z_count) for j in range(z_count)])
            )
        got = jnp.stack(blocks)
        if c == 0:
            ids = got[:, :, chunk].astype(jnp.int32)
            got = got[:, :, :chunk]
        hidden = got.astype(jnp.float32)[:, None] + ctx[:, :, None, cols]
        squares = squares + jnp.sum(hidden * hidden, axis=-1)
        flat = got.reshape(z_count * slots, chunk)
        y_own = y_own + dot_nt(flat, heads_own[:, cols])
        y_other = y_other + dot_nt(flat, heads_other[:, cols])
        b_own = b_own + dot_nt(ctx_pieces[:, cols], heads_own[:, cols])
        b_other = b_other + dot_nt(ctx_pieces[:, cols], heads_other[:, cols])

    scale = lax.rsqrt(squares / width + 1e-06)
    by_cond = weight[:, None] * scale[:, 0]
    by_uncond = (1.0 - weight)[:, None] * scale[:, 1]

    def finish(y, b, heads):
        shift = jnp.sum(heads[:, width : width + 3].astype(jnp.float32), axis=1)
        y = y.reshape(z_count, slots, group * feats)
        b = jnp.sum(b.reshape(3, z_count, 2, group * feats), axis=0)
        full = (
            (by_cond + by_uncond)[:, :, None] * y
            + by_cond[:, :, None] * b[:, 0][:, None]
            + by_uncond[:, :, None] * b[:, 1][:, None]
            + shift[None, None]
        ).reshape(z_count, slots, group, feats)
        hit = ids[:, :, None] == jnp.arange(group, dtype=jnp.int32)[None, None]
        return jnp.sum(jnp.where(hit[..., None], full, 0.0), axis=2)

    score_own = finish(y_own, b_own, heads_own)
    score_other = finish(y_other, b_other, heads_other)
    low = jnp.where(frame == 0, score_own, score_other)
    high = jnp.where(frame == 0, score_other, score_own)
    scored = jnp.concatenate([low, high], axis=2).astype(jnp.bfloat16)
    returned = [scored[0]]
    for d in range(1, z_count):
        returned.append(
            lax.ppermute(scored[d], "z", [(j, (j - d) % z_count) for j in range(z_count)])
        )
    flat_scores = jnp.concatenate(returned, axis=0)
    guided = dot_nn(jnp.transpose(picker), flat_scores).astype(jnp.bfloat16)
    return (jnp.concatenate(student, axis=1)[None, None], guided[None, None])


def solution(mesh):
    z_count, y_count, x_high, x_low = 4, 4, 2, mesh.shape["score"]
    fine = Mesh(
        mesh.devices.reshape(mesh.shape["frame"], z_count, y_count, x_high, x_low),
        ("frame", "z", "y", "xh", "xl"),
    )
    video = ("z", "y", "xh")
    scorer = ("z", "y", "xh", "xl")
    in_specs = (
        P("frame", video, None, "xl"),
        P("frame", video, None, "xl"),
        P("frame", video, None, "xl"),
        P("xl", None),
        P("frame", video, "xl", None),
        P("frame", video),
        P("frame", video, "xl", None),
        P(scorer, None, None),
        P(),
        P(),
        P(scorer, None, None),
    )
    out_specs = (P("frame", video, "xl", None), P("frame", video, "xl", None))
    return jax.shard_map(shards, mesh=fine, in_specs=in_specs, out_specs=out_specs, check_vma=False)
```

```python
import functools
import math

import jax
import jax.numpy as jnp
from jax import lax
from jax.experimental import pallas as pl
from jax.experimental.pallas import tpu as pltpu
from jax.sharding import Mesh
from jax.sharding import PartitionSpec as P

HEAD_DIM = 128
CHUNKS = 4
HEAD_GROUP = 5
SCALE2 = HEAD_DIM ** (-0.5) * math.log2(math.e)
NT = (((1,), (1,)), ((), ()))
NN = (((1,), (0,)), ((), ()))
MIB = 1024 * 1024
CAP = 8
BF16 = jnp.bfloat16
F32 = jnp.float32


def dot_nt(a, b):
    return lax.dot_general(a, b, NT, preferred_element_type=F32)


def dot_nn(a, b):
    return lax.dot_general(a, b, NN, preferred_element_type=F32)


def params(mib=24):
    return pltpu.CompilerParams(vmem_limit_bytes=mib * MIB)


def cost(flops, moved):
    return pl.CostEstimate(flops=flops, bytes_accessed=moved, transcendentals=0)


def attend_kernel(info, q_ref, k_ref, v_ref, ke_ref, ve_ref, *refs):
    o_ref = refs[-1]
    later = info[1] == 1

    @pl.when(later)
    def both():
        for h in range(HEAD_GROUP):
            cols = slice(h * HEAD_DIM, (h + 1) * HEAD_DIM)
            q = q_ref[:, cols]
            s_own = dot_nt(q, k_ref[:, cols])
            s_early = dot_nt(q, ke_ref[:, cols])
            peak = jnp.maximum(
                jnp.max(s_own, axis=1, keepdims=True), jnp.max(s_early, axis=1, keepdims=True)
            )
            p_own = jnp.exp2((s_own - peak) * SCALE2)
            p_early = jnp.exp2((s_early - peak) * SCALE2)
            total = jnp.sum(p_own, axis=1, keepdims=True) + jnp.sum(p_early, axis=1, keepdims=True)
            acc = dot_nn(p_own.astype(BF16), v_ref[:, cols]) + dot_nn(
                p_early.astype(BF16), ve_ref[:, cols]
            )
            o_ref[:, cols] = (acc / total).astype(BF16)

    @pl.when(jnp.logical_not(later))
    def own():
        for h in range(HEAD_GROUP):
            cols = slice(h * HEAD_DIM, (h + 1) * HEAD_DIM)
            s_own = dot_nt(q_ref[:, cols], k_ref[:, cols])
            peak = jnp.max(s_own, axis=1, keepdims=True)
            p_own = jnp.exp2((s_own - peak) * SCALE2)
            total = jnp.sum(p_own, axis=1, keepdims=True)
            acc = dot_nn(p_own.astype(BF16), v_ref[:, cols])
            o_ref[:, cols] = (acc / total).astype(BF16)


def attend(half, frame, queries, keys, values, keys_early, values_early, earlier=()):
    tok, width = queries.shape
    rows = tok // 2
    wide = HEAD_GROUP * HEAD_DIM
    whole = pl.BlockSpec((tok, wide), lambda i, info: (0, i))
    early = pl.BlockSpec((tok, wide), lambda i, info: (0, i * info[1]))
    return pl.pallas_call(
        attend_kernel,
        grid_spec=pltpu.PrefetchScalarGridSpec(
            num_scalar_prefetch=1,
            grid=(width // wide,),
            in_specs=[pl.BlockSpec((rows, wide), lambda i, info: (info[0], i))]
            + [whole] * 2
            + [early] * 2
            + [pl.BlockSpec(memory_space=pl.ANY)] * len(earlier),
            out_specs=pl.BlockSpec((rows, wide), lambda i, info: (0, i)),
        ),
        out_shape=jax.ShapeDtypeStruct((rows, width), BF16),
        compiler_params=params(56),
        cost_estimate=cost(8 * rows * tok * width, 5 * tok * width * 2),
        name="attend",
    )(
        jnp.stack([half, frame]).astype(jnp.int32),
        queries,
        keys,
        values,
        keys_early,
        values_early,
        *earlier,
    )


def project_kernel(a_ref, w_ref, *refs):
    refs[-1][...] = dot_nn(a_ref[...], w_ref[...]).astype(BF16)


def project(a, w, start, count, earlier=(), tile=640):
    rows, depth = a.shape
    first = start // tile
    return pl.pallas_call(
        project_kernel,
        grid=(count // tile,),
        in_specs=[
            pl.BlockSpec((rows, depth), lambda i: (0, 0)),
            pl.BlockSpec((depth, tile), lambda i: (0, first + i)),
        ]
        + [pl.BlockSpec(memory_space=pl.ANY)] * len(earlier),
        out_specs=pl.BlockSpec((rows, tile), lambda i: (0, i)),
        out_shape=jax.ShapeDtypeStruct((rows, count), BF16),
        compiler_params=params(56),
        cost_estimate=cost(2 * rows * depth * count, depth * count * 2),
        name="project",
    )(a, w, *earlier)


def combine_kernel(groups, level, kept_ref, got_ref, noise_ref, picker_ref, *refs):
    rows_ref, picked = refs[-1 - groups], refs[-groups:]
    rows = (kept_ref[...].astype(F32) + got_ref[...].astype(F32)).astype(BF16)
    rows_ref[...] = rows
    s = level[0]
    noisy = ((1.0 - s) * rows.astype(F32) + s * noise_ref[...].astype(F32)).astype(BF16)
    slots = picked[0].shape[0]
    for d, ref in enumerate(picked):
        ref[...] = dot_nn(picker_ref[d * slots : (d + 1) * slots, :], noisy).astype(BF16)


def combine(level, kept, got, noise, picker, buffer, earlier, start, groups, tile=640):
    rows, count = got.shape
    first = start // tile
    places = picker.shape[0]
    slots = places // groups
    at = pl.BlockSpec((rows, tile), lambda i, s: (0, first + i))
    local = pl.BlockSpec((rows, tile), lambda i, s: (0, i))
    out = pl.BlockSpec((slots, tile), lambda i, s: (0, i))
    rest = ([] if buffer is None else [buffer]) + list(earlier)
    result = pl.pallas_call(
        functools.partial(combine_kernel, groups),
        grid_spec=pltpu.PrefetchScalarGridSpec(
            num_scalar_prefetch=1,
            grid=(count // tile,),
            in_specs=[
                at,
                local,
                at,
                pl.BlockSpec((places, rows), lambda i, s: (0, 0)),
            ]
            + [pl.BlockSpec(memory_space=pl.ANY)] * len(rest),
            out_specs=[at] + [out] * groups,
        ),
        out_shape=[jax.ShapeDtypeStruct(kept.shape, BF16)]
        + [jax.ShapeDtypeStruct((slots, count), BF16)] * groups,
        input_output_aliases={} if buffer is None else {5: 0},
        compiler_params=params(),
        cost_estimate=cost(2 * rows * places * count, rows * count * 10),
        name="combine",
    )(level, kept, got, noise, picker, *rest)
    return result[0], list(result[1:])


def teach_kernel(groups, feats, width, first, last, *refs):
    refs = list(refs)
    weight = refs[0]
    xs = refs[1 : 1 + groups]
    heads_ref, pieces_ref, ctx_ref = refs[1 + groups : 4 + groups]
    at = 4 + groups
    if not first:
        y_in, sq_in = refs[at : at + 2]
        at += 2
    if last:
        ids = refs[at : at + groups]
        shift_ref = refs[at + groups]
        at += groups + 1
        outs = refs[at : at + groups]
        y_ref, sq_ref = refs[at + groups :]
    else:
        y_ref, sq_ref = refs[at:]
    slots = xs[0].shape[0]
    tile = xs[0].shape[1]
    half = heads_ref.shape[0] // 2
    step = pl.program_id(0)

    @pl.when(step == 0)
    def start():
        if first:
            y_ref[...] = jnp.zeros_like(y_ref)
            sq_ref[...] = jnp.zeros_like(sq_ref)
        else:
            y_ref[...] = y_in[...]
            sq_ref[...] = sq_in[...]

    flat = jnp.concatenate([x[...] for x in xs] + [pieces_ref[...]], axis=0)
    y_ref[...] += dot_nt(flat, heads_ref[...])
    for d in range(groups):
        for c in range(2):
            total = sq_ref[c, d * slots : (d + 1) * slots, :]
            for j in range(tile // 128):
                cols = slice(j * 128, (j + 1) * 128)
                hidden = xs[d][:, cols].astype(F32) + ctx_ref[2 * d + c : 2 * d + c + 1, cols]
                total = total + hidden * hidden
            sq_ref[c, d * slots : (d + 1) * slots, :] = total

    if last:

        @pl.when(step == pl.num_programs(0) - 1)
        def finish():
            rows = groups * slots
            lane = lax.broadcasted_iota(jnp.int32, (8, 128), 1)
            ones = jnp.where(lane < 3, 1.0, 0.0).astype(BF16)
            shift = dot_nt(ones, shift_ref[...])[0:1]
            feat = lax.rem(lax.broadcasted_iota(jnp.int32, (half, 2 * feats), 0), feats)
            column = lax.broadcasted_iota(jnp.int32, (half, 2 * feats), 1)
            scorer = lax.broadcasted_iota(jnp.int32, (slots, half), 1) // feats
            for d in range(groups):
                at_rows = slice(d * slots, (d + 1) * slots)
                scale = [
                    lax.rsqrt(
                        jnp.sum(sq_ref[c, at_rows, :], axis=1, keepdims=True) / width + 1e-06
                    )
                    for c in range(2)
                ]
                w = weight[d]
                by_cond = w * scale[0]
                by_uncond = (1.0 - w) * scale[1]
                hit = ids[d][:, 0:1].astype(F32).astype(jnp.int32) == scorer
                result = jnp.zeros((slots, 2 * feats), F32)
                for part in range(2):
                    lanes = slice(part * half, (part + 1) * half)
                    bias = [
                        sum(
                            y_ref[
                                rows + p * 2 * groups + 2 * d + c : rows + p * 2 * groups + 2 * d + c + 1,
                                lanes,
                            ]
                            for p in range(3)
                        )
                        for c in range(2)
                    ]
                    full = (
                        (by_cond + by_uncond) * y_ref[at_rows, lanes]
                        + by_cond * bias[0]
                        + by_uncond * bias[1]
                        + shift[:, lanes]
                    )
                    full = jnp.where(hit, full, 0.0)
                    gather = jnp.where(feat + part * feats == column, 1.0, 0.0).astype(BF16)
                    high = full.astype(BF16)
                    low = (full - high.astype(F32)).astype(BF16)
                    result = result + dot_nn(high, gather) + dot_nn(low, gather)
                outs[d][...] = result.astype(BF16)


def teach(weight, xs, heads, pieces, ctx, carry, ids, start, feats, width, last, tile=640):
    groups = len(xs)
    slots, count = xs[0].shape
    half = heads.shape[0] // 2
    first = start // tile
    rows = groups * slots + pieces.shape[0]
    shapes = [
        jax.ShapeDtypeStruct((rows, 2 * half), F32),
        jax.ShapeDtypeStruct((2, groups * slots, 128), F32),
    ]
    fixed = [
        pl.BlockSpec((rows, 2 * half), lambda i, *s: (0, 0)),
        pl.BlockSpec((2, groups * slots, 128), lambda i, *s: (0, 0, 0)),
    ]

    def at(height):
        return pl.BlockSpec((height, tile), lambda i, *s: (0, first + i))

    in_specs = [pl.BlockSpec((slots, tile), lambda i, *s: (0, i))] * groups
    in_specs += [at(2 * half), at(pieces.shape[0]), at(ctx.shape[0])]
    operands = [weight, *xs, heads, pieces, ctx]
    if carry is not None:
        in_specs += fixed
        operands += list(carry)
    scratch = []
    if last:
        in_specs += [pl.BlockSpec((slots, 128), lambda i, *s: (0, 0))] * groups
        in_specs += [pl.BlockSpec((2 * half, 128), lambda i, *s: (0, width // 128))]
        operands += [*ids, heads]
        out_specs = [pl.BlockSpec((slots, 2 * feats), lambda i, *s: (0, 0))] * groups
        out_shape = [jax.ShapeDtypeStruct((slots, 2 * feats), BF16)] * groups
        scratch = [pltpu.VMEM(s.shape, s.dtype) for s in shapes]
    else:
        out_specs = fixed
        out_shape = shapes
    return pl.pallas_call(
        functools.partial(teach_kernel, groups, feats, width, carry is None, last),
        grid_spec=pltpu.PrefetchScalarGridSpec(
            num_scalar_prefetch=1,
            grid=(count // tile,),
            in_specs=in_specs,
            out_specs=out_specs,
            scratch_shapes=scratch,
        ),
        out_shape=out_shape,
        compiler_params=params(),
        cost_estimate=cost(4 * rows * half * count, 4 * half * count + 8 * rows * half),
        name="teach",
    )(*operands)


def unpick_kernel(picker_ref, *refs):
    slots = refs[0].shape[0]
    total = 0.0
    for d, ref in enumerate(refs[:-1]):
        total = total + dot_nn(picker_ref[:, d * slots : (d + 1) * slots], ref[...])
    refs[-1][...] = total.astype(BF16)


def unpick(picker_back, scores):
    rows = picker_back.shape[0]
    return pl.pallas_call(
        unpick_kernel,
        out_shape=jax.ShapeDtypeStruct((rows, scores[0].shape[1]), BF16),
        compiler_params=params(),
        name="unpick",
    )(picker_back, *scores)


def split3(x):
    high = lax.reduce_precision(x, 8, 7)
    rest = x - high
    mid = lax.reduce_precision(rest, 8, 7)
    low = rest - mid
    return high.astype(BF16), mid.astype(BF16), low.astype(BF16)


def shards(
    queries,
    key_states,
    value_states,
    out_proj,
    noise_field,
    timesteps,
    routes,
    modulation,
    context,
    guidance,
    head_proj,
):
    frame = lax.axis_index("frame")
    xl = lax.axis_index("xl")
    xh = lax.axis_index("xh")
    y_at = lax.axis_index("y")
    z_at = lax.axis_index("z")
    z_count = lax.axis_size("z")
    y_count = lax.axis_size("y")
    x_count = lax.axis_size("xh") * lax.axis_size("xl")
    q, k, v = queries[0, 0], key_states[0, 0], value_states[0, 0]
    width = out_proj.shape[1]
    half_rows = q.shape[0] // 2
    chunk = width // CHUNKS
    swap = [(0, 1), (1, 0)]

    def along(axis, count, d):
        return [(j, (j + d) % count) for j in range(count)]

    k_early = lax.ppermute(k, "frame", [(0, 1)])
    v_early = lax.ppermute(v, "frame", [(0, 1)])

    head = head_proj[0].astype(F32)
    feats = head.shape[1] // 2
    scaled = jnp.transpose(head * (1.0 + modulation[0, 0])[:, None]).astype(BF16)
    shift_out = jnp.sum(head * modulation[0, 1][:, None], axis=0)
    extra = jnp.pad(jnp.stack(split3(shift_out), axis=1), ((0, 0), (0, 125)))
    packed = jnp.concatenate([scaled, extra], axis=1)
    mine = lax.dynamic_slice_in_dim(packed, frame * feats, feats, 0)
    heads = lax.all_gather(mine, ("frame", "y", "xh", "xl"), axis=0, tiled=True)
    group = x_count * y_count

    targets = routes[0, 0, :, 0]
    towards = lax.rem(targets // group - z_at + z_count, z_count)
    scorer_y = lax.rem(targets // x_count, y_count)
    local = scorer_y * x_count + lax.rem(targets, x_count)
    slots = group * CAP
    same = towards[:, None] == towards[None, :]
    at = jnp.arange(half_rows, dtype=jnp.int32)
    rank = jnp.sum((same & (at[:, None] > at[None, :])).astype(jnp.int32), axis=1)
    place = towards * slots + rank
    places = jnp.arange(z_count * slots, dtype=jnp.int32)
    picker = (place[None, :] == places[:, None]).astype(BF16)
    picker_back = (place[:, None] == places[None, :]).astype(BF16)
    tags = jnp.where(place[None, :] == places[:, None], local.astype(F32)[None, :], 0.0)
    tags = jnp.pad(jnp.sum(tags, axis=1).astype(BF16)[:, None], ((0, 0), (0, 127)))
    tags = tags.reshape(z_count, slots, 128)
    ids = [tags[0]] + [
        lax.ppermute(tags[d], "z", along("z", z_count, d)) for d in range(1, z_count)
    ]

    z_from = [lax.rem(z_at - d + z_count, z_count) for d in range(z_count)]
    videos = jnp.stack([(z * y_count + y_at) * lax.axis_size("xh") + xh for z in z_from])
    ctx = context[videos].reshape(2 * z_count, width)
    weight = guidance[videos]
    pieces = jnp.pad(jnp.concatenate(split3(ctx), axis=0), ((0, 8), (0, 0)))
    level = timesteps[0].astype(F32) / 1000.0

    part_far = attend(1 - xl, frame, q, k, v, k_early, v_early)
    sent = []
    for c in range(CHUNKS):
        sent.append(project(part_far, out_proj, c * chunk, chunk, sent[-1:]))
    arrived = [lax.ppermute(one, "xl", swap) for one in sent]
    part_own = attend(xl, frame, q, k, v, k_early, v_early, sent[-1:])
    kept = project(part_own, out_proj, 0, width)

    student = None
    carry = None
    done = []
    for c in range(CHUNKS):
        student, blocks = combine(
            level,
            kept,
            arrived[c],
            noise_field[0, 0],
            picker,
            student,
            done[c - 2 : c - 1] if c > 1 else [],
            c * chunk,
            z_count,
        )
        got = [blocks[0]] + [
            lax.ppermute(blocks[d], "z", along("z", z_count, d)) for d in range(1, z_count)
        ]
        carry = teach(
            weight, got, heads, pieces, ctx, carry, ids, c * chunk, feats, width, c == CHUNKS - 1
        )
        done.append(carry[0])
    returned = [carry[0]] + [
        lax.ppermute(carry[d], "z", along("z", z_count, z_count - d)) for d in range(1, z_count)
    ]
    guided = unpick(picker_back, returned)
    return (student[None, None], guided[None, None])


def solution(mesh):
    z_count, y_count, x_high, x_low = 4, 4, 2, mesh.shape["score"]
    fine = Mesh(
        mesh.devices.reshape(mesh.shape["frame"], z_count, y_count, x_high, x_low),
        ("frame", "z", "y", "xh", "xl"),
    )
    video = ("z", "y", "xh")
    scorer = ("z", "y", "xh", "xl")
    in_specs = (
        P("frame", video, None, "xl"),
        P("frame", video, None, "xl"),
        P("frame", video, None, "xl"),
        P("xl", None),
        P("frame", video, "xl", None),
        P("frame", video),
        P("frame", video, "xl", None),
        P(scorer, None, None),
        P(),
        P(),
        P(scorer, None, None),
    )
    out_specs = (P("frame", video, "xl", None), P("frame", video, "xl", None))
    return jax.shard_map(shards, mesh=fine, in_specs=in_specs, out_specs=out_specs, check_vma=False)
```

```python
import functools
import math

import jax
import jax.numpy as jnp
from jax import lax
from jax.experimental import pallas as pl
from jax.experimental.pallas import tpu as pltpu
from jax.sharding import Mesh
from jax.sharding import PartitionSpec as P

HEAD_DIM = 128
TILE = 640
PIECES = (1920, 1920, 1280)
HEAD_GROUP = 5
SCALE2 = HEAD_DIM ** (-0.5) * math.log2(math.e)
NT = (((1,), (1,)), ((), ()))
NN = (((1,), (0,)), ((), ()))
MIB = 1024 * 1024
CAP = 8
BF16 = jnp.bfloat16
F32 = jnp.float32


def dot_nt(a, b):
    return lax.dot_general(a, b, NT, preferred_element_type=F32)


def dot_nn(a, b):
    return lax.dot_general(a, b, NN, preferred_element_type=F32)


def params(mib=24):
    return pltpu.CompilerParams(vmem_limit_bytes=mib * MIB)


def cost(flops, moved):
    return pl.CostEstimate(flops=flops, bytes_accessed=moved, transcendentals=0)


def after(x, *earlier):
    def kernel(*refs):
        pass

    anywhere = pl.BlockSpec(memory_space=pl.ANY)
    return pl.pallas_call(
        kernel,
        in_specs=[anywhere] * (1 + len(earlier)),
        out_specs=anywhere,
        out_shape=jax.ShapeDtypeStruct(x.shape, x.dtype),
        input_output_aliases={0: 0},
        name="after",
    )(x, *earlier)


def attend_own_kernel(q_ref, k_ref, v_ref, o_ref, stat_ref):
    for h in range(HEAD_GROUP):
        cols = slice(h * HEAD_DIM, (h + 1) * HEAD_DIM)
        scores = dot_nt(q_ref[:, cols], k_ref[:, cols])
        peak = jnp.max(scores, axis=1, keepdims=True)
        weights = jnp.exp2((scores - peak) * SCALE2)
        total = jnp.sum(weights, axis=1, keepdims=True)
        acc = dot_nn(weights.astype(BF16), v_ref[:, cols])
        o_ref[:, cols] = (acc / total).astype(BF16)
        stat_ref[:, cols] = jnp.broadcast_to(peak * SCALE2 + jnp.log2(total), acc.shape)


def attend_own(queries, keys, values):
    tok, width = queries.shape
    wide = HEAD_GROUP * HEAD_DIM
    block = pl.BlockSpec((tok, wide), lambda i: (0, i))
    return pl.pallas_call(
        attend_own_kernel,
        grid=(width // wide,),
        in_specs=[block] * 3,
        out_specs=[block] * 2,
        out_shape=[
            jax.ShapeDtypeStruct((tok, width), BF16),
            jax.ShapeDtypeStruct((tok, width), F32),
        ],
        compiler_params=params(56),
        cost_estimate=cost(8 * tok * tok * width, 4 * tok * width * 2),
        name="attend_own",
    )(queries, keys, values)


def attend_early_kernel(info, q_ref, k_ref, v_ref, own_ref, stat_ref, o_ref):
    @pl.when(info[0] == 0)
    def keep():
        o_ref[...] = own_ref[...]

    @pl.when(info[0] == 1)
    def merge():
        for h in range(HEAD_GROUP):
            cols = slice(h * HEAD_DIM, (h + 1) * HEAD_DIM)
            scores = dot_nt(q_ref[:, cols], k_ref[:, cols])
            peak = jnp.max(scores, axis=1, keepdims=True)
            weights = jnp.exp2((scores - peak) * SCALE2)
            total = jnp.sum(weights, axis=1, keepdims=True)
            acc = dot_nn(weights.astype(BF16), v_ref[:, cols])
            gap = stat_ref[:, cols] - (peak * SCALE2 + jnp.log2(total))
            share_own = 1.0 / (1.0 + jnp.exp2(-gap))
            share_early = 1.0 / (1.0 + jnp.exp2(gap))
            merged = share_own * own_ref[:, cols].astype(F32) + (share_early / total) * acc
            o_ref[:, cols] = merged.astype(BF16)


def attend_early(frame, queries, keys, values, own, stats):
    tok, width = queries.shape
    wide = HEAD_GROUP * HEAD_DIM
    block = pl.BlockSpec((tok, wide), lambda i, info: (0, i * info[0]))
    return pl.pallas_call(
        attend_early_kernel,
        grid_spec=pltpu.PrefetchScalarGridSpec(
            num_scalar_prefetch=1,
            grid=(width // wide,),
            in_specs=[block] * 5,
            out_specs=block,
        ),
        out_shape=jax.ShapeDtypeStruct((tok, width), BF16),
        input_output_aliases={4: 0},
        compiler_params=params(56),
        cost_estimate=cost(8 * tok * tok * width, 5 * tok * width * 2),
        name="attend_early",
    )(frame.astype(jnp.int32).reshape(1), queries, keys, values, own, stats)


def project_kernel(counts, info, a_ref, w_ref, *refs):
    pieces = len(counts)
    fars, owns = refs[-2 * pieces : -pieces], refs[-pieces:]
    rows = fars[0].shape[0]
    tile = w_ref.shape[1]
    product = dot_nn(a_ref[...], w_ref[...]).astype(BF16)
    first = info[0] == 0
    own = jnp.where(first, product[:rows], product[rows:])
    far = jnp.where(first, product[rows:], product[:rows])
    step = 0
    for c, count in enumerate(counts):
        for j in range(count // tile):

            @pl.when(pl.program_id(0) == step)
            def store():
                owns[c][:, j * tile : (j + 1) * tile] = own
                fars[c][:, j * tile : (j + 1) * tile] = far

            step += 1


def project(half, a, w, start, counts, earlier=(), tile=TILE):
    rows, depth = a.shape
    first = start // tile
    total = sum(counts)
    outs = [pl.BlockSpec((rows // 2, count), lambda i, s: (0, 0)) for count in counts]
    shapes = [jax.ShapeDtypeStruct((rows // 2, count), BF16) for count in counts]
    result = pl.pallas_call(
        functools.partial(project_kernel, counts),
        grid_spec=pltpu.PrefetchScalarGridSpec(
            num_scalar_prefetch=1,
            grid=(total // tile,),
            in_specs=[
                pl.BlockSpec((rows, depth), lambda i, s: (0, 0)),
                pl.BlockSpec((depth, tile), lambda i, s: (0, first + i)),
            ]
            + [pl.BlockSpec(memory_space=pl.ANY)] * len(earlier),
            out_specs=outs * 2,
        ),
        out_shape=shapes * 2,
        compiler_params=params(56),
        cost_estimate=cost(2 * rows * depth * total, depth * total * 2),
        name="project",
    )(half.astype(jnp.int32).reshape(1), a, w, *earlier)
    return list(result[: len(counts)]), list(result[len(counts) :])


def combine_kernel(groups, steps, tagged, level, kept_ref, got_ref, noise_ref, picker_ref, *refs):
    rows_ref, picked = refs[-1 - groups], refs[-groups:]
    tile = kept_ref.shape[1]
    slots = picked[0].shape[0]
    rows = (kept_ref[...].astype(F32) + got_ref[...].astype(F32)).astype(BF16)
    rows_ref[...] = rows
    s = level[0]
    noisy = ((1.0 - s) * rows.astype(F32) + s * noise_ref[...].astype(F32)).astype(BF16)
    placed = dot_nn(picker_ref[...], noisy).astype(BF16)
    for j in range(steps):

        @pl.when(pl.program_id(0) == j)
        def store():
            for d, ref in enumerate(picked):
                at_rows = slice(d * slots, (d + 1) * slots)
                ref[:, j * tile : (j + 1) * tile] = placed[at_rows]
                if tagged and j == 0:
                    ref[:, steps * tile :] = refs[0][at_rows, :]


def combine(level, kept, got, noise, picker, buffer, tags, earlier, start, groups, tile=TILE):
    rows, count = got.shape
    width = noise.shape[1]
    first = start // tile
    places = picker.shape[0]
    steps = count // tile
    at = pl.BlockSpec((rows, tile), lambda i, s: (0, first + i))
    local = pl.BlockSpec((rows, tile), lambda i, s: (0, i))
    in_specs = [local, local, at, pl.BlockSpec((places, rows), lambda i, s: (0, 0))]
    operands = [level, kept, got, noise, picker]
    out_width = count
    if tags is not None:
        in_specs.append(pl.BlockSpec(tags.shape, lambda i, s: (0, 0)))
        operands.append(tags)
        out_width = count + tags.shape[1]
    rest = ([] if buffer is None else [buffer]) + list(earlier)
    block = (places // groups, out_width)
    result = pl.pallas_call(
        functools.partial(combine_kernel, groups, steps, tags is not None),
        grid_spec=pltpu.PrefetchScalarGridSpec(
            num_scalar_prefetch=1,
            grid=(steps,),
            in_specs=in_specs + [pl.BlockSpec(memory_space=pl.ANY)] * len(rest),
            out_specs=[at] + [pl.BlockSpec(block, lambda i, s: (0, 0))] * groups,
        ),
        out_shape=[jax.ShapeDtypeStruct((rows, width), BF16)]
        + [jax.ShapeDtypeStruct(block, BF16)] * groups,
        input_output_aliases={} if buffer is None else {len(operands): 0},
        compiler_params=params(50),
        cost_estimate=cost(1024, 1024),
        name="combine",
    )(*operands, *rest)
    return result[0], list(result[1:])


def teach_kernel(groups, feats, width, first, last, skip, *refs):
    refs = list(refs)
    weight = refs[0]
    xs = refs[1 : 1 + groups]
    heads_ref, pieces_ref, ctx_ref = refs[1 + groups : 4 + groups]
    at = 4 + groups
    if not first:
        y_in, sq_in = refs[at : at + 2]
        at += 2
    at += skip
    if last:
        ids = refs[at : at + groups]
        shift_ref = refs[at + groups]
        at += groups + 1
        outs = refs[at : at + groups]
        y_ref, sq_ref = refs[at + groups :]
    else:
        y_ref, sq_ref = refs[at:]
    slots = xs[0].shape[0]
    tile = xs[0].shape[1]
    half = heads_ref.shape[0] // 2
    step = pl.program_id(0)

    @pl.when(step == 0)
    def start():
        if first:
            y_ref[...] = jnp.zeros_like(y_ref)
            sq_ref[...] = jnp.zeros_like(sq_ref)
        else:
            y_ref[...] = y_in[...]
            sq_ref[...] = sq_in[...]

    flat = jnp.concatenate([x[...] for x in xs] + [pieces_ref[...]], axis=0)
    y_ref[...] += dot_nt(flat, heads_ref[...])
    for d in range(groups):
        for c in range(2):
            total = sq_ref[c, d * slots : (d + 1) * slots, :]
            for j in range(tile // 128):
                cols = slice(j * 128, (j + 1) * 128)
                hidden = xs[d][:, cols].astype(F32) + ctx_ref[2 * d + c : 2 * d + c + 1, cols]
                total = total + hidden * hidden
            sq_ref[c, d * slots : (d + 1) * slots, :] = total

    if last:

        @pl.when(step == pl.num_programs(0) - 1)
        def finish():
            rows = groups * slots
            lane = lax.broadcasted_iota(jnp.int32, (8, 128), 1)
            ones = jnp.where(lane < 3, 1.0, 0.0).astype(BF16)
            shift = dot_nt(ones, shift_ref[...])[0:1]
            feat = lax.rem(lax.broadcasted_iota(jnp.int32, (half, 2 * feats), 0), feats)
            column = lax.broadcasted_iota(jnp.int32, (half, 2 * feats), 1)
            scorer = lax.broadcasted_iota(jnp.int32, (slots, half), 1) // feats
            for d in range(groups):
                at_rows = slice(d * slots, (d + 1) * slots)
                scale = [
                    lax.rsqrt(
                        jnp.sum(sq_ref[c, at_rows, :], axis=1, keepdims=True) / width + 1e-06
                    )
                    for c in range(2)
                ]
                w = weight[d]
                by_cond = w * scale[0]
                by_uncond = (1.0 - w) * scale[1]
                hit = ids[d][:, 0:1].astype(F32).astype(jnp.int32) == scorer
                result = jnp.zeros((slots, 2 * feats), F32)
                for part in range(2):
                    lanes = slice(part * half, (part + 1) * half)
                    bias = [
                        sum(
                            y_ref[
                                rows + p * 2 * groups + 2 * d + c : rows + p * 2 * groups + 2 * d + c + 1,
                                lanes,
                            ]
                            for p in range(3)
                        )
                        for c in range(2)
                    ]
                    full = (
                        (by_cond + by_uncond) * y_ref[at_rows, lanes]
                        + by_cond * bias[0]
                        + by_uncond * bias[1]
                        + shift[:, lanes]
                    )
                    full = jnp.where(hit, full, 0.0)
                    gather = jnp.where(feat + part * feats == column, 1.0, 0.0).astype(BF16)
                    high = full.astype(BF16)
                    low = (full - high.astype(F32)).astype(BF16)
                    result = result + dot_nn(high, gather) + dot_nn(low, gather)
                outs[d][...] = result.astype(BF16)


def teach(
    weight, xs, heads, pieces, ctx, carry, ids, start, count, feats, width, last, earlier, tile=TILE
):
    groups = len(xs)
    slots = xs[0].shape[0]
    half = heads.shape[0] // 2
    first = start // tile
    rows = groups * slots + pieces.shape[0]
    shapes = [
        jax.ShapeDtypeStruct((rows, 2 * half), F32),
        jax.ShapeDtypeStruct((2, groups * slots, 128), F32),
    ]
    fixed = [
        pl.BlockSpec((rows, 2 * half), lambda i, *s: (0, 0)),
        pl.BlockSpec((2, groups * slots, 128), lambda i, *s: (0, 0, 0)),
    ]

    def at(height):
        return pl.BlockSpec((height, tile), lambda i, *s: (0, first + i))

    in_specs = [pl.BlockSpec((slots, tile), lambda i, *s: (0, i))] * groups
    in_specs += [at(2 * half), at(pieces.shape[0]), at(ctx.shape[0])]
    operands = [weight, *xs, heads, pieces, ctx]
    if carry is not None:
        in_specs += fixed
        operands += list(carry)
    in_specs += [pl.BlockSpec(memory_space=pl.ANY)] * len(earlier)
    operands += list(earlier)
    scratch = []
    if last:
        in_specs += [pl.BlockSpec((slots, 128), lambda i, *s: (0, PIECES[0] // 128))] * groups
        in_specs += [pl.BlockSpec((2 * half, 128), lambda i, *s: (0, width // 128))]
        operands += [*ids, heads]
        out_specs = [pl.BlockSpec((slots, 2 * feats), lambda i, *s: (0, 0))] * groups
        out_shape = [jax.ShapeDtypeStruct((slots, 2 * feats), BF16)] * groups
        scratch = [pltpu.VMEM(s.shape, s.dtype) for s in shapes]
    else:
        out_specs = fixed
        out_shape = shapes
    return pl.pallas_call(
        functools.partial(teach_kernel, groups, feats, width, carry is None, last, len(earlier)),
        grid_spec=pltpu.PrefetchScalarGridSpec(
            num_scalar_prefetch=1,
            grid=(count // tile,),
            in_specs=in_specs,
            out_specs=out_specs,
            scratch_shapes=scratch,
        ),
        out_shape=out_shape,
        compiler_params=params(50),
        cost_estimate=cost(1024, 1024),
        name="teach",
    )(*operands)


def unpick_kernel(picker_ref, *refs):
    slots = refs[0].shape[0]
    total = 0.0
    for d, ref in enumerate(refs[:-1]):
        total = total + dot_nn(picker_ref[:, d * slots : (d + 1) * slots], ref[...])
    refs[-1][...] = total.astype(BF16)


def unpick(picker_back, scores):
    rows = picker_back.shape[0]
    return pl.pallas_call(
        unpick_kernel,
        out_shape=jax.ShapeDtypeStruct((rows, scores[0].shape[1]), BF16),
        compiler_params=params(),
        name="unpick",
    )(picker_back, *scores)


def split3(x):
    high = lax.reduce_precision(x, 8, 7)
    rest = x - high
    mid = lax.reduce_precision(rest, 8, 7)
    low = rest - mid
    return high.astype(BF16), mid.astype(BF16), low.astype(BF16)


def shards(
    queries,
    key_states,
    value_states,
    out_proj,
    noise_field,
    timesteps,
    routes,
    modulation,
    context,
    guidance,
    head_proj,
):
    frame = lax.axis_index("frame")
    xl = lax.axis_index("xl")
    xh = lax.axis_index("xh")
    y_at = lax.axis_index("y")
    z_at = lax.axis_index("z")
    z_count = lax.axis_size("z")
    y_count = lax.axis_size("y")
    x_count = lax.axis_size("xh") * lax.axis_size("xl")
    q, k, v = queries[0, 0], key_states[0, 0], value_states[0, 0]
    width = out_proj.shape[1]
    half_rows = q.shape[0] // 2
    starts = [sum(PIECES[:c]) for c in range(len(PIECES))]
    swap = [(0, 1), (1, 0)]

    def along(count, d):
        return [(j, (j + d) % count) for j in range(count)]

    k_early = lax.ppermute(k, "frame", [(0, 1)])
    v_early = lax.ppermute(v, "frame", [(0, 1)])

    head = head_proj[0].astype(F32)
    feats = head.shape[1] // 2
    scaled = jnp.transpose(head * (1.0 + modulation[0, 0])[:, None]).astype(BF16)
    shift_out = jnp.sum(head * modulation[0, 1][:, None], axis=0)
    extra = jnp.pad(jnp.stack(split3(shift_out), axis=1), ((0, 0), (0, 125)))
    packed = jnp.concatenate([scaled, extra], axis=1)
    mine = lax.dynamic_slice_in_dim(packed, frame * feats, feats, 0)
    heads_x = lax.all_gather(mine, ("xh", "xl"), axis=0, tiled=True)
    group = x_count * y_count

    targets = routes[0, 0, :, 0]
    towards = lax.rem(targets // group - z_at + z_count, z_count)
    scorer_y = lax.rem(targets // x_count, y_count)
    local = scorer_y * x_count + lax.rem(targets, x_count)
    slots = group * CAP
    same = towards[:, None] == towards[None, :]
    at = jnp.arange(half_rows, dtype=jnp.int32)
    rank = jnp.sum((same & (at[:, None] > at[None, :])).astype(jnp.int32), axis=1)
    place = towards * slots + rank
    places = jnp.arange(z_count * slots, dtype=jnp.int32)
    picker = (place[None, :] == places[:, None]).astype(BF16)
    picker_back = (place[:, None] == places[None, :]).astype(BF16)
    tags = jnp.where(place[None, :] == places[:, None], local.astype(F32)[None, :], 0.0)
    tags = jnp.pad(jnp.sum(tags, axis=1).astype(BF16)[:, None], ((0, 0), (0, 127)))

    z_from = [lax.rem(z_at - d + z_count, z_count) for d in range(z_count)]
    videos = jnp.stack([(z * y_count + y_at) * lax.axis_size("xh") + xh for z in z_from])
    ctx = context[videos].reshape(2 * z_count, width)
    weight = guidance[videos]
    pieces = jnp.pad(jnp.concatenate(split3(ctx), axis=0), ((0, 8), (0, 0)))
    level = timesteps[0].astype(F32) / 1000.0

    attended, stats = attend_own(q, k, v)
    attended = attend_early(frame, q, k_early, v_early, attended, stats)
    sent, kept = project(xl, attended, out_proj, 0, PIECES[:1])
    heads = lax.all_gather(after(heads_x, *kept), ("frame", "y"), axis=0, tiled=True)
    far, own = project(xl, attended, out_proj, PIECES[0], PIECES[1:], sent)
    sent, kept = sent + far, kept + own
    arrived = [lax.ppermute(sent[0], "xl", swap), lax.ppermute(sent[1], "xl", swap)]
    arrived.append(lax.ppermute(after(sent[2], arrived[1]), "xl", swap))

    student = None
    carry = None
    got = []

    def send(c, earlier):
        student_now, blocks = combine(
            level,
            kept[c],
            arrived[c],
            noise_field[0, 0],
            picker,
            student,
            tags if c == 0 else None,
            earlier,
            starts[c],
            z_count,
        )
        got.append(
            [blocks[0]]
            + [lax.ppermute(blocks[d], "z", along(z_count, d)) for d in range(1, z_count)]
        )
        return student_now

    def score(c, earlier):
        return teach(
            weight,
            got[c],
            heads,
            pieces,
            ctx,
            carry,
            got[0],
            starts[c],
            PIECES[c],
            feats,
            width,
            c == len(PIECES) - 1,
            earlier,
        )

    student = send(0, [])
    student = send(1, [])
    carry = score(0, got[1][:1])
    student = send(2, carry[:1])
    carry = score(1, got[2][:1])
    carry = score(2, [])
    returned = [carry[0]] + [
        lax.ppermute(carry[d], "z", along(z_count, z_count - d)) for d in range(1, z_count)
    ]
    guided = unpick(picker_back, returned)
    return (student[None, None], guided[None, None])


def solution(mesh):
    z_count, y_count, x_high, x_low = 4, 4, 2, mesh.shape["score"]
    fine = Mesh(
        mesh.devices.reshape(mesh.shape["frame"], z_count, y_count, x_high, x_low),
        ("frame", "z", "y", "xh", "xl"),
    )
    video = ("z", "y", "xh")
    scorer = ("z", "y", "xh", "xl")
    in_specs = (
        P("frame", video, None, "xl"),
        P("frame", video, None, "xl"),
        P("frame", video, None, "xl"),
        P("xl", None),
        P("frame", video, "xl", None),
        P("frame", video),
        P("frame", video, "xl", None),
        P(scorer, None, None),
        P(),
        P(),
        P(scorer, None, None),
    )
    out_specs = (P("frame", video, "xl", None), P("frame", video, "xl", None))
    return jax.shard_map(shards, mesh=fine, in_specs=in_specs, out_specs=out_specs, check_vma=False)
```

```python
import functools
import math

import jax
import jax.numpy as jnp
from jax import lax
from jax.experimental import pallas as pl
from jax.experimental.pallas import tpu as pltpu
from jax.sharding import Mesh
from jax.sharding import PartitionSpec as P

HEAD_DIM = 128
TILE = 640
PIECES = (1920, 1920, 1280)
HEAD_GROUP = 5
SCALE2 = HEAD_DIM ** (-0.5) * math.log2(math.e)
NT = (((1,), (1,)), ((), ()))
NN = (((1,), (0,)), ((), ()))
MIB = 1024 * 1024
CAP = 8
BF16 = jnp.bfloat16
F32 = jnp.float32


def dot_nt(a, b):
    return lax.dot_general(a, b, NT, preferred_element_type=F32)


def dot_nn(a, b):
    return lax.dot_general(a, b, NN, preferred_element_type=F32)


def params(mib=24):
    return pltpu.CompilerParams(vmem_limit_bytes=mib * MIB)


def cost(flops, moved):
    return pl.CostEstimate(flops=flops, bytes_accessed=moved, transcendentals=0)


def after(x, *earlier):
    def kernel(*refs):
        pass

    anywhere = pl.BlockSpec(memory_space=pl.ANY)
    return pl.pallas_call(
        kernel,
        in_specs=[anywhere] * (1 + len(earlier)),
        out_specs=anywhere,
        out_shape=jax.ShapeDtypeStruct(x.shape, x.dtype),
        input_output_aliases={0: 0},
        name="after",
    )(x, *earlier)


def attend_own_kernel(q_ref, k_ref, v_ref, o_ref, stat_ref):
    for h in range(HEAD_GROUP):
        cols = slice(h * HEAD_DIM, (h + 1) * HEAD_DIM)
        scores = dot_nt(q_ref[:, cols], k_ref[:, cols])
        peak = jnp.max(scores, axis=1, keepdims=True)
        weights = jnp.exp2((scores - peak) * SCALE2)
        total = jnp.sum(weights, axis=1, keepdims=True)
        acc = dot_nn(weights.astype(BF16), v_ref[:, cols])
        o_ref[:, cols] = (acc / total).astype(BF16)
        stat_ref[:, cols] = jnp.broadcast_to(peak * SCALE2 + jnp.log2(total), acc.shape)


def attend_own(queries, keys, values):
    tok, width = queries.shape
    wide = HEAD_GROUP * HEAD_DIM
    block = pl.BlockSpec((tok, wide), lambda i: (0, i))
    return pl.pallas_call(
        attend_own_kernel,
        grid=(width // wide,),
        in_specs=[block] * 3,
        out_specs=[block] * 2,
        out_shape=[
            jax.ShapeDtypeStruct((tok, width), BF16),
            jax.ShapeDtypeStruct((tok, width), F32),
        ],
        compiler_params=params(56),
        cost_estimate=cost(8 * tok * tok * width, 4 * tok * width * 2),
        name="attend_own",
    )(queries, keys, values)


def attend_early_kernel(info, q_ref, k_ref, v_ref, own_ref, stat_ref, o_ref):
    @pl.when(info[0] == 0)
    def keep():
        o_ref[...] = own_ref[...]

    @pl.when(info[0] == 1)
    def merge():
        for h in range(HEAD_GROUP):
            cols = slice(h * HEAD_DIM, (h + 1) * HEAD_DIM)
            scores = dot_nt(q_ref[:, cols], k_ref[:, cols])
            peak = jnp.max(scores, axis=1, keepdims=True)
            weights = jnp.exp2((scores - peak) * SCALE2)
            total = jnp.sum(weights, axis=1, keepdims=True)
            acc = dot_nn(weights.astype(BF16), v_ref[:, cols])
            gap = stat_ref[:, cols] - (peak * SCALE2 + jnp.log2(total))
            share_own = 1.0 / (1.0 + jnp.exp2(-gap))
            share_early = 1.0 / (1.0 + jnp.exp2(gap))
            merged = share_own * own_ref[:, cols].astype(F32) + (share_early / total) * acc
            o_ref[:, cols] = merged.astype(BF16)


def attend_early(frame, queries, keys, values, own, stats):
    tok, width = queries.shape
    wide = HEAD_GROUP * HEAD_DIM
    block = pl.BlockSpec((tok, wide), lambda i, info: (0, i * info[0]))
    return pl.pallas_call(
        attend_early_kernel,
        grid_spec=pltpu.PrefetchScalarGridSpec(
            num_scalar_prefetch=1,
            grid=(width // wide,),
            in_specs=[block] * 5,
            out_specs=block,
        ),
        out_shape=jax.ShapeDtypeStruct((tok, width), BF16),
        input_output_aliases={4: 0},
        compiler_params=params(56),
        cost_estimate=cost(8 * tok * tok * width, 5 * tok * width * 2),
        name="attend_early",
    )(frame.astype(jnp.int32).reshape(1), queries, keys, values, own, stats)


def project_kernel(counts, info, a_ref, w_ref, *refs):
    pieces = len(counts)
    fars, owns = refs[-2 * pieces : -pieces], refs[-pieces:]
    rows = fars[0].shape[0]
    tile = w_ref.shape[1]
    product = dot_nn(a_ref[...], w_ref[...]).astype(BF16)
    first = info[0] == 0
    own = jnp.where(first, product[:rows], product[rows:])
    far = jnp.where(first, product[rows:], product[:rows])
    step = 0
    for c, count in enumerate(counts):
        for j in range(count // tile):

            @pl.when(pl.program_id(0) == step)
            def store():
                owns[c][:, j * tile : (j + 1) * tile] = own
                fars[c][:, j * tile : (j + 1) * tile] = far

            step += 1


def project(half, a, w, start, counts, earlier=(), tile=TILE):
    rows, depth = a.shape
    first = start // tile
    total = sum(counts)
    outs = [pl.BlockSpec((rows // 2, count), lambda i, s: (0, 0)) for count in counts]
    shapes = [jax.ShapeDtypeStruct((rows // 2, count), BF16) for count in counts]
    result = pl.pallas_call(
        functools.partial(project_kernel, counts),
        grid_spec=pltpu.PrefetchScalarGridSpec(
            num_scalar_prefetch=1,
            grid=(total // tile,),
            in_specs=[
                pl.BlockSpec((rows, depth), lambda i, s: (0, 0)),
                pl.BlockSpec((depth, tile), lambda i, s: (0, first + i)),
            ]
            + [pl.BlockSpec(memory_space=pl.ANY)] * len(earlier),
            out_specs=outs * 2,
        ),
        out_shape=shapes * 2,
        compiler_params=params(56),
        cost_estimate=cost(2 * rows * depth * total, depth * total * 2),
        name="project",
    )(half.astype(jnp.int32).reshape(1), a, w, *earlier)
    return list(result[: len(counts)]), list(result[len(counts) :])


def combine_kernel(groups, steps, tagged, level, kept_ref, got_ref, noise_ref, picker_ref, *refs):
    rows_ref, picked = refs[-1 - groups], refs[-groups:]
    tile = kept_ref.shape[1]
    slots = picked[0].shape[0]
    rows = (kept_ref[...].astype(F32) + got_ref[...].astype(F32)).astype(BF16)
    rows_ref[...] = rows
    s = level[0]
    noisy = ((1.0 - s) * rows.astype(F32) + s * noise_ref[...].astype(F32)).astype(BF16)
    placed = dot_nn(picker_ref[...], noisy).astype(BF16)
    for j in range(steps):

        @pl.when(pl.program_id(0) == j)
        def store():
            for d, ref in enumerate(picked):
                at_rows = slice(d * slots, (d + 1) * slots)
                ref[:, j * tile : (j + 1) * tile] = placed[at_rows]
                if tagged and j == 0:
                    ref[:, steps * tile :] = refs[0][at_rows, :]


def combine(level, kept, got, noise, picker, buffer, tags, earlier, start, groups, tile=TILE):
    rows, count = got.shape
    width = noise.shape[1]
    first = start // tile
    places = picker.shape[0]
    steps = count // tile
    at = pl.BlockSpec((rows, tile), lambda i, s: (0, first + i))
    local = pl.BlockSpec((rows, tile), lambda i, s: (0, i))
    in_specs = [local, local, at, pl.BlockSpec((places, rows), lambda i, s: (0, 0))]
    operands = [level, kept, got, noise, picker]
    out_width = count
    if tags is not None:
        in_specs.append(pl.BlockSpec(tags.shape, lambda i, s: (0, 0)))
        operands.append(tags)
        out_width = count + tags.shape[1]
    rest = ([] if buffer is None else [buffer]) + list(earlier)
    block = (places // groups, out_width)
    result = pl.pallas_call(
        functools.partial(combine_kernel, groups, steps, tags is not None),
        grid_spec=pltpu.PrefetchScalarGridSpec(
            num_scalar_prefetch=1,
            grid=(steps,),
            in_specs=in_specs + [pl.BlockSpec(memory_space=pl.ANY)] * len(rest),
            out_specs=[at] + [pl.BlockSpec(block, lambda i, s: (0, 0))] * groups,
        ),
        out_shape=[jax.ShapeDtypeStruct((rows, width), BF16)]
        + [jax.ShapeDtypeStruct(block, BF16)] * groups,
        input_output_aliases={} if buffer is None else {len(operands): 0},
        compiler_params=params(50),
        cost_estimate=cost(1024, 1024),
        name="combine",
    )(*operands, *rest)
    return result[0], list(result[1:])


def teach_kernel(groups, feats, width, first, last, skip, *refs):
    refs = list(refs)
    weight = refs[0]
    xs = refs[1 : 1 + groups]
    heads_ref, pieces_ref, ctx_ref = refs[1 + groups : 4 + groups]
    at = 4 + groups
    if not first:
        y_in, sq_in = refs[at : at + 2]
        at += 2
    at += skip
    if last:
        ids = refs[at : at + groups]
        shift_ref = refs[at + groups]
        at += groups + 1
        outs = refs[at : at + groups]
        y_ref, sq_ref = refs[at + groups :]
    else:
        y_ref, sq_ref = refs[at:]
    slots = xs[0].shape[0]
    tile = xs[0].shape[1]
    half = heads_ref.shape[0] // 2
    step = pl.program_id(0)

    @pl.when(step == 0)
    def start():
        if first:
            y_ref[...] = jnp.zeros_like(y_ref)
            sq_ref[...] = jnp.zeros_like(sq_ref)
        else:
            y_ref[...] = y_in[...]
            sq_ref[...] = sq_in[...]

    flat = jnp.concatenate([x[...] for x in xs] + [pieces_ref[...]], axis=0)
    y_ref[...] += dot_nt(flat, heads_ref[...])
    for d in range(groups):
        for c in range(2):
            total = sq_ref[c, d * slots : (d + 1) * slots, :]
            for j in range(tile // 128):
                cols = slice(j * 128, (j + 1) * 128)
                hidden = xs[d][:, cols].astype(F32) + ctx_ref[2 * d + c : 2 * d + c + 1, cols]
                total = total + hidden * hidden
            sq_ref[c, d * slots : (d + 1) * slots, :] = total

    if last:

        @pl.when(step == pl.num_programs(0) - 1)
        def finish():
            rows = groups * slots
            lane = lax.broadcasted_iota(jnp.int32, (8, 128), 1)
            ones = jnp.where(lane < 3, 1.0, 0.0).astype(BF16)
            shift = dot_nt(ones, shift_ref[...])[0:1]
            feat = lax.rem(lax.broadcasted_iota(jnp.int32, (half, 2 * feats), 0), feats)
            column = lax.broadcasted_iota(jnp.int32, (half, 2 * feats), 1)
            scorer = lax.broadcasted_iota(jnp.int32, (slots, half), 1) // feats
            for d in range(groups):
                at_rows = slice(d * slots, (d + 1) * slots)
                scale = [
                    lax.rsqrt(
                        jnp.sum(sq_ref[c, at_rows, :], axis=1, keepdims=True) / width + 1e-06
                    )
                    for c in range(2)
                ]
                w = weight[d]
                by_cond = w * scale[0]
                by_uncond = (1.0 - w) * scale[1]
                hit = ids[d][:, 0:1].astype(F32).astype(jnp.int32) == scorer
                result = jnp.zeros((slots, 2 * feats), F32)
                for part in range(2):
                    lanes = slice(part * half, (part + 1) * half)
                    bias = [
                        sum(
                            y_ref[
                                rows + p * 2 * groups + 2 * d + c : rows + p * 2 * groups + 2 * d + c + 1,
                                lanes,
                            ]
                            for p in range(3)
                        )
                        for c in range(2)
                    ]
                    full = (
                        (by_cond + by_uncond) * y_ref[at_rows, lanes]
                        + by_cond * bias[0]
                        + by_uncond * bias[1]
                        + shift[:, lanes]
                    )
                    full = jnp.where(hit, full, 0.0)
                    gather = jnp.where(feat + part * feats == column, 1.0, 0.0).astype(BF16)
                    high = full.astype(BF16)
                    low = (full - high.astype(F32)).astype(BF16)
                    result = result + dot_nn(high, gather) + dot_nn(low, gather)
                outs[d][...] = result.astype(BF16)


def teach(
    weight, xs, heads, pieces, ctx, carry, ids, start, count, feats, width, last, earlier, tile=TILE
):
    groups = len(xs)
    slots = xs[0].shape[0]
    half = heads.shape[0] // 2
    first = start // tile
    rows = groups * slots + pieces.shape[0]
    shapes = [
        jax.ShapeDtypeStruct((rows, 2 * half), F32),
        jax.ShapeDtypeStruct((2, groups * slots, 128), F32),
    ]
    fixed = [
        pl.BlockSpec((rows, 2 * half), lambda i, *s: (0, 0)),
        pl.BlockSpec((2, groups * slots, 128), lambda i, *s: (0, 0, 0)),
    ]

    def at(height):
        return pl.BlockSpec((height, tile), lambda i, *s: (0, first + i))

    in_specs = [pl.BlockSpec((slots, tile), lambda i, *s: (0, i))] * groups
    in_specs += [at(2 * half), at(pieces.shape[0]), at(ctx.shape[0])]
    operands = [weight, *xs, heads, pieces, ctx]
    if carry is not None:
        in_specs += fixed
        operands += list(carry)
    in_specs += [pl.BlockSpec(memory_space=pl.ANY)] * len(earlier)
    operands += list(earlier)
    scratch = []
    if last:
        in_specs += [pl.BlockSpec((slots, 128), lambda i, *s: (0, PIECES[0] // 128))] * groups
        in_specs += [pl.BlockSpec((2 * half, 128), lambda i, *s: (0, width // 128))]
        operands += [*ids, heads]
        out_specs = [pl.BlockSpec((slots, 2 * feats), lambda i, *s: (0, 0))] * groups
        out_shape = [jax.ShapeDtypeStruct((slots, 2 * feats), BF16)] * groups
        scratch = [pltpu.VMEM(s.shape, s.dtype) for s in shapes]
    else:
        out_specs = fixed
        out_shape = shapes
    return pl.pallas_call(
        functools.partial(teach_kernel, groups, feats, width, carry is None, last, len(earlier)),
        grid_spec=pltpu.PrefetchScalarGridSpec(
            num_scalar_prefetch=1,
            grid=(count // tile,),
            in_specs=in_specs,
            out_specs=out_specs,
            scratch_shapes=scratch,
        ),
        out_shape=out_shape,
        compiler_params=params(50),
        cost_estimate=cost(1024, 1024),
        name="teach",
    )(*operands)


def unpick_kernel(picker_ref, *refs):
    slots = refs[0].shape[0]
    total = 0.0
    for d, ref in enumerate(refs[:-1]):
        total = total + dot_nn(picker_ref[:, d * slots : (d + 1) * slots], ref[...])
    refs[-1][...] = total.astype(BF16)


def unpick(picker_back, scores):
    rows = picker_back.shape[0]
    return pl.pallas_call(
        unpick_kernel,
        out_shape=jax.ShapeDtypeStruct((rows, scores[0].shape[1]), BF16),
        compiler_params=params(),
        name="unpick",
    )(picker_back, *scores)


def split3(x):
    high = lax.reduce_precision(x, 8, 7)
    rest = x - high
    mid = lax.reduce_precision(rest, 8, 7)
    low = rest - mid
    return high.astype(BF16), mid.astype(BF16), low.astype(BF16)


def shards(
    queries,
    key_states,
    value_states,
    out_proj,
    noise_field,
    timesteps,
    routes,
    modulation,
    context,
    guidance,
    head_proj,
):
    frame = lax.axis_index("frame")
    xl = lax.axis_index("xl")
    xh = lax.axis_index("xh")
    y_at = lax.axis_index("y")
    z_at = lax.axis_index("z")
    z_count = lax.axis_size("z")
    y_count = lax.axis_size("y")
    x_count = lax.axis_size("xh") * lax.axis_size("xl")
    q, k, v = queries[0, 0], key_states[0, 0], value_states[0, 0]
    width = out_proj.shape[1]
    half_rows = q.shape[0] // 2
    starts = [sum(PIECES[:c]) for c in range(len(PIECES))]
    swap = [(0, 1), (1, 0)]

    def along(count, d):
        return [(j, (j + d) % count) for j in range(count)]

    k_early = lax.ppermute(k, "frame", [(0, 1)])
    v_early = lax.ppermute(v, "frame", [(0, 1)])

    head = head_proj[0].astype(F32)
    feats = head.shape[1] // 2
    scaled = jnp.transpose(head * (1.0 + modulation[0, 0])[:, None]).astype(BF16)
    shift_out = jnp.sum(head * modulation[0, 1][:, None], axis=0)
    extra = jnp.pad(jnp.stack(split3(shift_out), axis=1), ((0, 0), (0, 125)))
    packed = jnp.concatenate([scaled, extra], axis=1)
    mine = lax.dynamic_slice_in_dim(packed, frame * feats, feats, 0)
    heads_x = lax.all_gather(mine, ("xh", "xl"), axis=0, tiled=True)
    group = x_count * y_count

    targets = routes[0, 0, :, 0]
    towards = lax.rem(targets // group - z_at + z_count, z_count)
    scorer_y = lax.rem(targets // x_count, y_count)
    local = scorer_y * x_count + lax.rem(targets, x_count)
    slots = group * CAP
    same = towards[:, None] == towards[None, :]
    at = jnp.arange(half_rows, dtype=jnp.int32)
    rank = jnp.sum((same & (at[:, None] > at[None, :])).astype(jnp.int32), axis=1)
    place = towards * slots + rank
    places = jnp.arange(z_count * slots, dtype=jnp.int32)
    picker = (place[None, :] == places[:, None]).astype(BF16)
    picker_back = (place[:, None] == places[None, :]).astype(BF16)
    tags = jnp.where(place[None, :] == places[:, None], local.astype(F32)[None, :], 0.0)
    tags = jnp.pad(jnp.sum(tags, axis=1).astype(BF16)[:, None], ((0, 0), (0, 127)))

    z_from = [lax.rem(z_at - d + z_count, z_count) for d in range(z_count)]
    videos = jnp.stack([(z * y_count + y_at) * lax.axis_size("xh") + xh for z in z_from])
    ctx = context[videos].reshape(2 * z_count, width)
    weight = guidance[videos]
    pieces = jnp.pad(jnp.concatenate(split3(ctx), axis=0), ((0, 8), (0, 0)))
    level = timesteps[0].astype(F32) / 1000.0

    attended, stats = attend_own(q, k, v)
    attended = attend_early(frame, q, k_early, v_early, attended, stats)
    sent, kept = project(xl, attended, out_proj, 0, PIECES[:1])
    heads = lax.all_gather(after(heads_x, *kept), ("frame", "y"), axis=0, tiled=True)
    far, own = project(xl, attended, out_proj, PIECES[0], PIECES[1:], sent)
    sent, kept = sent + far, kept + own
    arrived = [lax.ppermute(sent[0], "xl", swap), lax.ppermute(sent[1], "xl", swap)]
    arrived.append(lax.ppermute(after(sent[2], arrived[1]), "xl", swap))

    student = None
    carry = None
    got = []

    def send(c, earlier):
        student_now, blocks = combine(
            level,
            kept[c],
            arrived[c],
            noise_field[0, 0],
            picker,
            student,
            tags if c == 0 else None,
            earlier,
            starts[c],
            z_count,
        )
        got.append(
            [blocks[0]]
            + [lax.ppermute(blocks[d], "z", along(z_count, d)) for d in range(1, z_count)]
        )
        return student_now

    def score(c, earlier):
        return teach(
            weight,
            got[c],
            heads,
            pieces,
            ctx,
            carry,
            got[0],
            starts[c],
            PIECES[c],
            feats,
            width,
            c == len(PIECES) - 1,
            earlier,
        )

    student = send(0, [])
    student = send(1, [])
    student = send(2, got[0][1:])
    carry = score(0, got[2][:1])
    carry = score(1, [])
    carry = score(2, [])
    returned = [carry[0]] + [
        lax.ppermute(carry[d], "z", along(z_count, z_count - d)) for d in range(1, z_count)
    ]
    guided = unpick(picker_back, returned)
    return (student[None, None], guided[None, None])


def solution(mesh):
    z_count, y_count, x_high, x_low = 4, 4, 2, mesh.shape["score"]
    fine = Mesh(
        mesh.devices.reshape(mesh.shape["frame"], z_count, y_count, x_high, x_low),
        ("frame", "z", "y", "xh", "xl"),
    )
    video = ("z", "y", "xh")
    scorer = ("z", "y", "xh", "xl")
    in_specs = (
        P("frame", video, None, "xl"),
        P("frame", video, None, "xl"),
        P("frame", video, None, "xl"),
        P("xl", None),
        P("frame", video, "xl", None),
        P("frame", video),
        P("frame", video, "xl", None),
        P(scorer, None, None),
        P(),
        P(),
        P(scorer, None, None),
    )
    out_specs = (P("frame", video, "xl", None), P("frame", video, "xl", None))
    return jax.shard_map(shards, mesh=fine, in_specs=in_specs, out_specs=out_specs, check_vma=False)
```

```python
import functools
import math

import jax
import jax.numpy as jnp
from jax import lax
from jax.experimental import pallas as pl
from jax.experimental.pallas import tpu as pltpu
from jax.sharding import Mesh
from jax.sharding import PartitionSpec as P

HEAD_DIM = 128
TILE = 640
PIECES = (1920, 1920, 1280)
HEAD_GROUP = 5
SCALE2 = HEAD_DIM ** (-0.5) * math.log2(math.e)
NT = (((1,), (1,)), ((), ()))
NN = (((1,), (0,)), ((), ()))
MIB = 1024 * 1024
CAP = 8
BF16 = jnp.bfloat16
F32 = jnp.float32


def dot_nt(a, b):
    return lax.dot_general(a, b, NT, preferred_element_type=F32)


def dot_nn(a, b):
    return lax.dot_general(a, b, NN, preferred_element_type=F32)


def params(mib=24):
    return pltpu.CompilerParams(vmem_limit_bytes=mib * MIB)


def cost(flops, moved):
    return pl.CostEstimate(flops=flops, bytes_accessed=moved, transcendentals=0)


def after(x, *earlier):
    def kernel(*refs):
        pass

    anywhere = pl.BlockSpec(memory_space=pl.ANY)
    return pl.pallas_call(
        kernel,
        in_specs=[anywhere] * (1 + len(earlier)),
        out_specs=anywhere,
        out_shape=jax.ShapeDtypeStruct(x.shape, x.dtype),
        input_output_aliases={0: 0},
        name="after",
    )(x, *earlier)


def attend_own_kernel(q_ref, k_ref, v_ref, o_ref, stat_ref):
    for h in range(HEAD_GROUP):
        cols = slice(h * HEAD_DIM, (h + 1) * HEAD_DIM)
        scores = dot_nt(q_ref[:, cols], k_ref[:, cols])
        peak = jnp.max(scores, axis=1, keepdims=True)
        weights = jnp.exp2((scores - peak) * SCALE2)
        total = jnp.sum(weights, axis=1, keepdims=True)
        acc = dot_nn(weights.astype(BF16), v_ref[:, cols])
        o_ref[:, cols] = (acc / total).astype(BF16)
        stat_ref[:, cols] = jnp.broadcast_to(peak * SCALE2 + jnp.log2(total), acc.shape)


def attend_own(queries, keys, values):
    tok, width = queries.shape
    wide = HEAD_GROUP * HEAD_DIM
    block = pl.BlockSpec((tok, wide), lambda i: (0, i))
    return pl.pallas_call(
        attend_own_kernel,
        grid=(width // wide,),
        in_specs=[block] * 3,
        out_specs=[block] * 2,
        out_shape=[
            jax.ShapeDtypeStruct((tok, width), BF16),
            jax.ShapeDtypeStruct((tok, width), F32),
        ],
        compiler_params=params(56),
        cost_estimate=cost(8 * tok * tok * width, 4 * tok * width * 2),
        name="attend_own",
    )(queries, keys, values)


def attend_early_kernel(info, q_ref, k_ref, v_ref, own_ref, stat_ref, o_ref):
    @pl.when(info[0] == 0)
    def keep():
        o_ref[...] = own_ref[...]

    @pl.when(info[0] == 1)
    def merge():
        for h in range(HEAD_GROUP):
            cols = slice(h * HEAD_DIM, (h + 1) * HEAD_DIM)
            scores = dot_nt(q_ref[:, cols], k_ref[:, cols])
            peak = jnp.max(scores, axis=1, keepdims=True)
            weights = jnp.exp2((scores - peak) * SCALE2)
            total = jnp.sum(weights, axis=1, keepdims=True)
            acc = dot_nn(weights.astype(BF16), v_ref[:, cols])
            gap = stat_ref[:, cols] - (peak * SCALE2 + jnp.log2(total))
            share_own = 1.0 / (1.0 + jnp.exp2(-gap))
            early = acc / total
            merged = early + share_own * (own_ref[:, cols].astype(F32) - early)
            o_ref[:, cols] = merged.astype(BF16)


def attend_early(frame, queries, keys, values, own, stats):
    tok, width = queries.shape
    wide = HEAD_GROUP * HEAD_DIM
    block = pl.BlockSpec((tok, wide), lambda i, info: (0, i * info[0]))
    return pl.pallas_call(
        attend_early_kernel,
        grid_spec=pltpu.PrefetchScalarGridSpec(
            num_scalar_prefetch=1,
            grid=(width // wide,),
            in_specs=[block] * 5,
            out_specs=block,
        ),
        out_shape=jax.ShapeDtypeStruct((tok, width), BF16),
        input_output_aliases={4: 0},
        compiler_params=params(56),
        cost_estimate=cost(8 * tok * tok * width, 5 * tok * width * 2),
        name="attend_early",
    )(frame.astype(jnp.int32).reshape(1), queries, keys, values, own, stats)


def project_kernel(counts, info, a_ref, w_ref, *refs):
    pieces = len(counts)
    fars, owns = refs[-2 * pieces : -pieces], refs[-pieces:]
    rows = fars[0].shape[0]
    tile = w_ref.shape[1]
    product = dot_nn(a_ref[...], w_ref[...]).astype(BF16)
    first = info[0] == 0
    own = jnp.where(first, product[:rows], product[rows:])
    far = jnp.where(first, product[rows:], product[:rows])
    step = 0
    for c, count in enumerate(counts):
        for j in range(count // tile):

            @pl.when(pl.program_id(0) == step)
            def store():
                owns[c][:, j * tile : (j + 1) * tile] = own
                fars[c][:, j * tile : (j + 1) * tile] = far

            step += 1


def project(half, a, w, start, counts, earlier=(), tile=TILE):
    rows, depth = a.shape
    first = start // tile
    total = sum(counts)
    outs = [pl.BlockSpec((rows // 2, count), lambda i, s: (0, 0)) for count in counts]
    shapes = [jax.ShapeDtypeStruct((rows // 2, count), BF16) for count in counts]
    result = pl.pallas_call(
        functools.partial(project_kernel, counts),
        grid_spec=pltpu.PrefetchScalarGridSpec(
            num_scalar_prefetch=1,
            grid=(total // tile,),
            in_specs=[
                pl.BlockSpec((rows, depth), lambda i, s: (0, 0)),
                pl.BlockSpec((depth, tile), lambda i, s: (0, first + i)),
            ]
            + [pl.BlockSpec(memory_space=pl.ANY)] * len(earlier),
            out_specs=outs * 2,
        ),
        out_shape=shapes * 2,
        compiler_params=params(56),
        cost_estimate=cost(2 * rows * depth * total, depth * total * 2),
        name="project",
    )(half.astype(jnp.int32).reshape(1), a, w, *earlier)
    return list(result[: len(counts)]), list(result[len(counts) :])


def combine_kernel(groups, steps, tagged, level, kept_ref, got_ref, noise_ref, picker_ref, *refs):
    rows_ref, picked = refs[-1 - groups], refs[-groups:]
    tile = kept_ref.shape[1]
    slots = picked[0].shape[0]
    rows = (kept_ref[...].astype(F32) + got_ref[...].astype(F32)).astype(BF16)
    rows_ref[...] = rows
    s = level[0]
    noisy = ((1.0 - s) * rows.astype(F32) + s * noise_ref[...].astype(F32)).astype(BF16)
    placed = dot_nn(picker_ref[...], noisy).astype(BF16)
    for j in range(steps):

        @pl.when(pl.program_id(0) == j)
        def store():
            for d, ref in enumerate(picked):
                at_rows = slice(d * slots, (d + 1) * slots)
                ref[:, j * tile : (j + 1) * tile] = placed[at_rows]
                if tagged and j == 0:
                    ref[:, steps * tile :] = refs[0][at_rows, :]


def combine(level, kept, got, noise, picker, buffer, tags, earlier, start, groups, tile=TILE):
    rows, count = got.shape
    width = noise.shape[1]
    first = start // tile
    places = picker.shape[0]
    steps = count // tile
    at = pl.BlockSpec((rows, tile), lambda i, s: (0, first + i))
    local = pl.BlockSpec((rows, tile), lambda i, s: (0, i))
    in_specs = [local, local, at, pl.BlockSpec((places, rows), lambda i, s: (0, 0))]
    operands = [level, kept, got, noise, picker]
    out_width = count
    if tags is not None:
        in_specs.append(pl.BlockSpec(tags.shape, lambda i, s: (0, 0)))
        operands.append(tags)
        out_width = count + tags.shape[1]
    rest = ([] if buffer is None else [buffer]) + list(earlier)
    block = (places // groups, out_width)
    result = pl.pallas_call(
        functools.partial(combine_kernel, groups, steps, tags is not None),
        grid_spec=pltpu.PrefetchScalarGridSpec(
            num_scalar_prefetch=1,
            grid=(steps,),
            in_specs=in_specs + [pl.BlockSpec(memory_space=pl.ANY)] * len(rest),
            out_specs=[at] + [pl.BlockSpec(block, lambda i, s: (0, 0))] * groups,
        ),
        out_shape=[jax.ShapeDtypeStruct((rows, width), BF16)]
        + [jax.ShapeDtypeStruct(block, BF16)] * groups,
        input_output_aliases={} if buffer is None else {len(operands): 0},
        compiler_params=params(50),
        cost_estimate=cost(1024, 1024),
        name="combine",
    )(*operands, *rest)
    return result[0], list(result[1:])


def teach_kernel(groups, feats, width, first, last, skip, *refs):
    refs = list(refs)
    weight = refs[0]
    xs = refs[1 : 1 + groups]
    heads_ref, pieces_ref, ctx_ref = refs[1 + groups : 4 + groups]
    at = 4 + groups
    if not first:
        y_in, sq_in = refs[at : at + 2]
        at += 2
    at += skip
    if last:
        ids = refs[at : at + groups]
        shift_ref = refs[at + groups]
        at += groups + 1
        outs = refs[at : at + groups]
        y_ref, sq_ref = refs[at + groups :]
    else:
        y_ref, sq_ref = refs[at:]
    slots = xs[0].shape[0]
    tile = xs[0].shape[1]
    half = heads_ref.shape[0] // 2
    step = pl.program_id(0)

    @pl.when(step == 0)
    def start():
        if first:
            y_ref[...] = jnp.zeros_like(y_ref)
            sq_ref[...] = jnp.zeros_like(sq_ref)
        else:
            y_ref[...] = y_in[...]
            sq_ref[...] = sq_in[...]

    flat = jnp.concatenate([x[...] for x in xs] + [pieces_ref[...]], axis=0)
    y_ref[...] += dot_nt(flat, heads_ref[...])
    for d in range(groups):
        for c in range(2):
            total = sq_ref[c, d * slots : (d + 1) * slots, :]
            for j in range(tile // 128):
                cols = slice(j * 128, (j + 1) * 128)
                hidden = xs[d][:, cols].astype(F32) + ctx_ref[2 * d + c : 2 * d + c + 1, cols]
                total = total + hidden * hidden
            sq_ref[c, d * slots : (d + 1) * slots, :] = total

    if last:

        @pl.when(step == pl.num_programs(0) - 1)
        def finish():
            rows = groups * slots
            lane = lax.broadcasted_iota(jnp.int32, (8, 128), 1)
            ones = jnp.where(lane < 3, 1.0, 0.0).astype(BF16)
            shift = dot_nt(ones, shift_ref[...])[0:1]
            feat = lax.rem(lax.broadcasted_iota(jnp.int32, (half, 2 * feats), 0), feats)
            column = lax.broadcasted_iota(jnp.int32, (half, 2 * feats), 1)
            scorer = lax.broadcasted_iota(jnp.int32, (slots, half), 1) // feats
            for d in range(groups):
                at_rows = slice(d * slots, (d + 1) * slots)
                scale = [
                    lax.rsqrt(
                        jnp.sum(sq_ref[c, at_rows, :], axis=1, keepdims=True) / width + 1e-06
                    )
                    for c in range(2)
                ]
                w = weight[d]
                by_cond = w * scale[0]
                by_uncond = (1.0 - w) * scale[1]
                hit = ids[d][:, 0:1].astype(F32).astype(jnp.int32) == scorer
                result = jnp.zeros((slots, 2 * feats), F32)
                for part in range(2):
                    lanes = slice(part * half, (part + 1) * half)
                    bias = [
                        sum(
                            y_ref[
                                rows + p * 2 * groups + 2 * d + c : rows + p * 2 * groups + 2 * d + c + 1,
                                lanes,
                            ]
                            for p in range(3)
                        )
                        for c in range(2)
                    ]
                    full = (
                        (by_cond + by_uncond) * y_ref[at_rows, lanes]
                        + by_cond * bias[0]
                        + by_uncond * bias[1]
                        + shift[:, lanes]
                    )
                    full = jnp.where(hit, full, 0.0)
                    gather = jnp.where(feat + part * feats == column, 1.0, 0.0).astype(BF16)
                    high = full.astype(BF16)
                    low = (full - high.astype(F32)).astype(BF16)
                    result = result + dot_nn(high, gather) + dot_nn(low, gather)
                outs[d][...] = result.astype(BF16)


def teach(
    weight, xs, heads, pieces, ctx, carry, ids, start, count, feats, width, last, earlier, tile=TILE
):
    groups = len(xs)
    slots = xs[0].shape[0]
    half = heads.shape[0] // 2
    first = start // tile
    rows = groups * slots + pieces.shape[0]
    shapes = [
        jax.ShapeDtypeStruct((rows, 2 * half), F32),
        jax.ShapeDtypeStruct((2, groups * slots, 128), F32),
    ]
    fixed = [
        pl.BlockSpec((rows, 2 * half), lambda i, *s: (0, 0)),
        pl.BlockSpec((2, groups * slots, 128), lambda i, *s: (0, 0, 0)),
    ]

    def at(height):
        return pl.BlockSpec((height, tile), lambda i, *s: (0, first + i))

    in_specs = [pl.BlockSpec((slots, tile), lambda i, *s: (0, i))] * groups
    in_specs += [at(2 * half), at(pieces.shape[0]), at(ctx.shape[0])]
    operands = [weight, *xs, heads, pieces, ctx]
    if carry is not None:
        in_specs += fixed
        operands += list(carry)
    in_specs += [pl.BlockSpec(memory_space=pl.ANY)] * len(earlier)
    operands += list(earlier)
    scratch = []
    if last:
        in_specs += [pl.BlockSpec((slots, 128), lambda i, *s: (0, PIECES[0] // 128))] * groups
        in_specs += [pl.BlockSpec((2 * half, 128), lambda i, *s: (0, width // 128))]
        operands += [*ids, heads]
        out_specs = [pl.BlockSpec((slots, 2 * feats), lambda i, *s: (0, 0))] * groups
        out_shape = [jax.ShapeDtypeStruct((slots, 2 * feats), BF16)] * groups
        scratch = [pltpu.VMEM(s.shape, s.dtype) for s in shapes]
    else:
        out_specs = fixed
        out_shape = shapes
    return pl.pallas_call(
        functools.partial(teach_kernel, groups, feats, width, carry is None, last, len(earlier)),
        grid_spec=pltpu.PrefetchScalarGridSpec(
            num_scalar_prefetch=1,
            grid=(count // tile,),
            in_specs=in_specs,
            out_specs=out_specs,
            scratch_shapes=scratch,
        ),
        out_shape=out_shape,
        compiler_params=params(50),
        cost_estimate=cost(1024, 1024),
        name="teach",
    )(*operands)


def unpick_kernel(picker_ref, *refs):
    slots = refs[0].shape[0]
    total = 0.0
    for d, ref in enumerate(refs[:-1]):
        total = total + dot_nn(picker_ref[:, d * slots : (d + 1) * slots], ref[...])
    refs[-1][...] = total.astype(BF16)


def unpick(picker_back, scores):
    rows = picker_back.shape[0]
    return pl.pallas_call(
        unpick_kernel,
        out_shape=jax.ShapeDtypeStruct((rows, scores[0].shape[1]), BF16),
        compiler_params=params(),
        name="unpick",
    )(picker_back, *scores)


def split3(x):
    high = lax.reduce_precision(x, 8, 7)
    rest = x - high
    mid = lax.reduce_precision(rest, 8, 7)
    low = rest - mid
    return high.astype(BF16), mid.astype(BF16), low.astype(BF16)


def shards(
    queries,
    key_states,
    value_states,
    out_proj,
    noise_field,
    timesteps,
    routes,
    modulation,
    context,
    guidance,
    head_proj,
):
    frame = lax.axis_index("frame")
    xl = lax.axis_index("xl")
    xh = lax.axis_index("xh")
    y_at = lax.axis_index("y")
    z_at = lax.axis_index("z")
    z_count = lax.axis_size("z")
    y_count = lax.axis_size("y")
    x_count = lax.axis_size("xh") * lax.axis_size("xl")
    q, k, v = queries[0, 0], key_states[0, 0], value_states[0, 0]
    width = out_proj.shape[1]
    half_rows = q.shape[0] // 2
    starts = [sum(PIECES[:c]) for c in range(len(PIECES))]
    swap = [(0, 1), (1, 0)]

    def along(count, d):
        return [(j, (j + d) % count) for j in range(count)]

    k_early = lax.ppermute(k, "frame", [(0, 1)])
    v_early = lax.ppermute(v, "frame", [(0, 1)])

    head = head_proj[0].astype(F32)
    feats = head.shape[1] // 2
    scaled = jnp.transpose(head * (1.0 + modulation[0, 0])[:, None]).astype(BF16)
    shift_out = jnp.sum(head * modulation[0, 1][:, None], axis=0)
    extra = jnp.pad(jnp.stack(split3(shift_out), axis=1), ((0, 0), (0, 125)))
    packed = jnp.concatenate([scaled, extra], axis=1)
    mine = lax.dynamic_slice_in_dim(packed, frame * feats, feats, 0)
    heads_x = lax.all_gather(mine, ("xh", "xl"), axis=0, tiled=True)
    group = x_count * y_count

    targets = routes[0, 0, :, 0]
    towards = lax.rem(targets // group - z_at + z_count, z_count)
    scorer_y = lax.rem(targets // x_count, y_count)
    local = scorer_y * x_count + lax.rem(targets, x_count)
    slots = group * CAP
    same = towards[:, None] == towards[None, :]
    at = jnp.arange(half_rows, dtype=jnp.int32)
    rank = jnp.sum((same & (at[:, None] > at[None, :])).astype(jnp.int32), axis=1)
    place = towards * slots + rank
    places = jnp.arange(z_count * slots, dtype=jnp.int32)
    picker = (place[None, :] == places[:, None]).astype(BF16)
    picker_back = (place[:, None] == places[None, :]).astype(BF16)
    tags = jnp.where(place[None, :] == places[:, None], local.astype(F32)[None, :], 0.0)
    tags = jnp.pad(jnp.sum(tags, axis=1).astype(BF16)[:, None], ((0, 0), (0, 127)))

    z_from = [lax.rem(z_at - d + z_count, z_count) for d in range(z_count)]
    videos = jnp.stack([(z * y_count + y_at) * lax.axis_size("xh") + xh for z in z_from])
    ctx = context[videos].reshape(2 * z_count, width)
    weight = guidance[videos]
    pieces = jnp.pad(jnp.concatenate(split3(ctx), axis=0), ((0, 8), (0, 0)))
    level = timesteps[0].astype(F32) / 1000.0

    attended, stats = attend_own(q, k, v)
    attended = attend_early(frame, q, k_early, v_early, attended, stats)
    sent, kept = project(xl, attended, out_proj, 0, PIECES[:1])
    heads = lax.all_gather(after(heads_x, *kept), ("frame", "y"), axis=0, tiled=True)
    far, own = project(xl, attended, out_proj, PIECES[0], PIECES[1:], sent)
    sent, kept = sent + far, kept + own
    arrived = [lax.ppermute(sent[0], "xl", swap), lax.ppermute(sent[1], "xl", swap)]
    arrived.append(lax.ppermute(after(sent[2], arrived[1]), "xl", swap))

    student = None
    carry = None
    got = []

    def send(c, earlier):
        student_now, blocks = combine(
            level,
            kept[c],
            arrived[c],
            noise_field[0, 0],
            picker,
            student,
            tags if c == 0 else None,
            earlier,
            starts[c],
            z_count,
        )
        got.append(
            [blocks[0]]
            + [lax.ppermute(blocks[d], "z", along(z_count, d)) for d in range(1, z_count)]
        )
        return student_now

    def score(c, earlier):
        return teach(
            weight,
            got[c],
            heads,
            pieces,
            ctx,
            carry,
            got[0],
            starts[c],
            PIECES[c],
            feats,
            width,
            c == len(PIECES) - 1,
            earlier,
        )

    student = send(0, [])
    student = send(1, [])
    student = send(2, got[0][1:])
    carry = score(0, got[2][:1])
    carry = score(1, [])
    carry = score(2, [])
    returned = [carry[0]] + [
        lax.ppermute(carry[d], "z", along(z_count, z_count - d)) for d in range(1, z_count)
    ]
    guided = unpick(picker_back, returned)
    return (student[None, None], guided[None, None])


def solution(mesh):
    z_count, y_count, x_high, x_low = 4, 4, 2, mesh.shape["score"]
    fine = Mesh(
        mesh.devices.reshape(mesh.shape["frame"], z_count, y_count, x_high, x_low),
        ("frame", "z", "y", "xh", "xl"),
    )
    video = ("z", "y", "xh")
    scorer = ("z", "y", "xh", "xl")
    in_specs = (
        P("frame", video, None, "xl"),
        P("frame", video, None, "xl"),
        P("frame", video, None, "xl"),
        P("xl", None),
        P("frame", video, "xl", None),
        P("frame", video),
        P("frame", video, "xl", None),
        P(scorer, None, None),
        P(),
        P(),
        P(scorer, None, None),
    )
    out_specs = (P("frame", video, "xl", None), P("frame", video, "xl", None))
    return jax.shard_map(shards, mesh=fine, in_specs=in_specs, out_specs=out_specs, check_vma=False)
```
